128 devices in a mesh: tm: 4 (over z), lat: 32 (over x, y, core).
Axes of the slice: x: 4, y: 4, z: 4, core: 2. Of those that a mesh axis runs over, the one named last changes fastest.
Arguments:
- forcing: float32 [4, 2, 137, 128, 128], P('tm', None, None, 'lat'), may hold values from -6 to 6
- coupling: float32 [137, 137], replicated, may hold values from -0.5 to 0.5
- diffusion: float32 [128, 128], P('lat'), may hold values from 0.02 to 0.12
- error_scale: float32 [137], replicated, may hold values from 0.3 to 3
- pick_cols: int32 [4, 32, 32, 16, 4], P('tm', 'lat'), may hold values from 0 to 511
- pick_weights: float32 [4, 32, 32, 16, 4], P('tm', 'lat'), may hold values from 0 to 1
- send_count: int32 [4, 32, 32], P('tm', 'lat'), may hold values from 1 to 16, 256 in all within a row
- jacobian: float32 [4, 32, 32, 16, 22, 137], P('tm', 'lat'), may hold values from -0.5 to 0.5
- obs_weight: float32 [4, 32, 32, 16, 22], P('tm', 'lat'), may hold values from 0.2 to 5
Outputs:
- gradient: float32 [4, 2, 137, 128, 128], P('tm', None, None, 'lat')
The draws below stay inside these ranges and needn't reach their ends.
Inputs may be any that keep to these rules, and one draw needn't show every extreme that they name: The first send_count slots of each source band to each owner are used, the rest are empty; the counts of one source band in one sub-window sum to 256.
All inputs are finite; a program needn't handle non-finite values.
Results may differ from the reference program's by a relative error of at most 0.0001.
Values sent between devices are 32-bit elements; how exact they have to be, the bound alone decides.
A program may use at most 128 MiB of HBM per device.

```python
import math
import jax
import jax.numpy as jnp
import numpy as np
from jax import lax

L = 137
CH = 22
LANCZOS = 2
STEPS = 4
NEAR = 4
CAP = 16
ROWS = 4
LON = 128
WINDOWS = 4
BANDS = 32
NR = 128


def place_ends(result, own_key, low, top_value):
    index_at = [jax.random.randint(jax.random.fold_in(own_key, axis), (), 0, length) for axis, length in enumerate(result.shape)]
    main_axis = result.shape.index(max(result.shape))
    beside = index_at[:main_axis] + [(index_at[main_axis] + 1) % result.shape[main_axis]] + index_at[main_axis + 1:]
    return result.at[tuple(index_at)].set(low).at[tuple(beside)].set(top_value)


def block_levels(own_key, shape, cuts, least, largest):
    factor_of, own = 1.0, jax.random.fold_in(own_key, 6)
    for dim, parts in cuts:
        heights = jnp.exp(jax.random.uniform(jax.random.fold_in(own, dim), (parts,), jnp.float32, least / len(cuts), largest / len(cuts)))
        factor_of = factor_of * jnp.repeat(heights, shape[dim] // parts).reshape([-1 if axis == dim else 1 for axis in range(len(shape))])
    return factor_of


def split_up(number_of, total, most, lean):
    loads = [(1 << 20) // math.isqrt(grade ** lean) + 1 for grade in range(2, number_of + 1)]
    surplus, given = total - most - (number_of - 1), [1] * (number_of - 1)
    while surplus > 0:
        candidates = [i for i in range(number_of - 1) if given[i] < most]
        whole, budget = sum([loads[i] for i in candidates]), surplus
        for i in candidates:
            more = min(most - given[i], max(1, budget * loads[i] // whole), surplus)
            given[i] = given[i] + more
            surplus = surplus - more
    return np.array([most] + given)


def uneven(own_key, count, total, limit, lean):
    if count == 2:
        one = jax.random.randint(own_key, (), max(1, total - limit), min(limit, total - 1) + 1)
        return jnp.stack([one, total - one])
    tallies = jnp.asarray(split_up(count, total, limit, lean), jnp.int32)
    couples = (count - 1) // 2
    giver, sink = tallies[1:1 + 2 * couples:2], tallies[2:2 + 2 * couples:2]
    slack = jnp.minimum(giver - 1, limit - sink)
    passed = jax.random.randint(jax.random.fold_in(own_key, 1), (couples,), 0, 1 << 20) % (slack + 1)
    tallies = tallies.at[1:1 + 2 * couples:2].set(giver - passed).at[2:2 + 2 * couples:2].set(sink + passed)
    return tallies[jax.random.permutation(jax.random.fold_in(own_key, 2), count)]


def bell_draw(rng, shape, deviation, most, shards=(), kind=jnp.bfloat16):
    values = deviation * jax.random.normal(rng, shape, jnp.float32)
    if shards:
        values = values * block_levels(rng, shape, shards, -0.22, 0.18)
    return jnp.clip(values, -most, most).astype(kind)


def setup_inputs(seed: int = 0) -> dict:
    keys = jax.random.split(jax.random.key(seed), 10)
    forcing = bell_draw(keys[0], (WINDOWS, LANCZOS, L, NR, LON), 1.0, 6.0, ((0, 4), (3, 32)), jnp.float32)
    coupling = bell_draw(keys[1], (L, L), L ** -0.5, 0.5, (), jnp.float32)
    diffusion = jnp.clip(jnp.exp(math.log(0.12) - 1.7917595 * jax.random.uniform(keys[2], (NR, LON), jnp.float32) ** block_levels(keys[2], (NR, LON), ((0, 32),), -0.2, 0.2)), 0.02, 0.12)
    error_scale = jnp.clip(jnp.exp(jax.random.uniform(keys[3], (L,), jnp.float32, math.log(0.3), math.log(3.0))), 0.3, 3.0)
    pick_cols = place_ends(jax.random.randint(keys[4], (WINDOWS, BANDS, BANDS, CAP, NEAR), 0, ROWS * LON), jax.random.fold_in(keys[4], 1), 0, (ROWS * LON) - 1).astype(jnp.int32)
    pick_weights = jnp.clip(1.0 * jax.random.uniform(keys[5], (WINDOWS, BANDS, BANDS, CAP, NEAR), jnp.float32) ** block_levels(keys[5], (WINDOWS, BANDS, BANDS, CAP, NEAR), ((0, 4), (1, 32)), -0.2, 0.2), 0.0, 1.0)
    send_count = jax.vmap(lambda own: uneven(own, BANDS, BANDS * CAP // 2, CAP, 2))(jax.random.split(keys[6], WINDOWS * BANDS)).reshape((WINDOWS, BANDS, BANDS)).astype(jnp.int32)
    jacobian = bell_draw(keys[7], (WINDOWS, BANDS, BANDS, CAP, CH, L), L ** -0.5, 0.5, ((0, 4), (1, 32)), jnp.float32)
    obs_weight = jnp.clip(jnp.exp(math.log(5.0) - 3.218876 * jax.random.uniform(keys[8], (WINDOWS, BANDS, BANDS, CAP, CH), jnp.float32) ** block_levels(keys[8], (WINDOWS, BANDS, BANDS, CAP, CH), ((0, 4), (1, 32)), -0.2, 0.2)), 0.2, 5.0)
    return {"forcing": forcing, "coupling": coupling, "diffusion": diffusion, "error_scale": error_scale, "pick_cols": pick_cols, "pick_weights": pick_weights, "send_count": send_count, "jacobian": jacobian, "obs_weight": obs_weight}


def laplace(field):
    padded = jnp.pad(field, ((0, 0), (0, 0), (1, 1), (0, 0)))
    return padded[:, :, 2:] + padded[:, :, :-2] + jnp.roll(field, 1, 3) + jnp.roll(field, -1, 3) - 4.0 * field


def forward(state, coupling, diffusion):
    mixed = 0.8 * state + 0.2 * jnp.einsum("kl,vlrc->vkrc", coupling, state, precision=lax.Precision.HIGHEST)
    return mixed + diffusion * laplace(mixed)


def backward(state, coupling, diffusion):
    summed = state + laplace(diffusion * state)
    return 0.8 * summed + 0.2 * jnp.einsum("lk,vlrc->vkrc", coupling, summed, precision=lax.Precision.HIGHEST)


def take_band(band_cols, columns):
    return band_cols[:, :, columns]


def put_band(columns, contrib):
    empty = jnp.zeros((contrib.shape[0], contrib.shape[1], ROWS * LON), jnp.float32)
    return empty.at[:, :, columns].add(contrib)


def observe(end_state, columns, weights, counts, jac_block, err_block):
    lanczos = end_state.shape[0]
    banded = end_state.reshape(lanczos, L, BANDS, ROWS * LON)
    slots = jnp.arange(CAP, dtype=jnp.int32)
    live_slots = (slots[None, None, :] < counts[:, :, None]).astype(jnp.float32)
    used_weights = weights * live_slots[..., None]
    gathered = jax.vmap(take_band, in_axes=(2, 0), out_axes=2)(banded, columns)
    profile = jnp.sum(gathered * used_weights[None, None], axis=-1)
    hidden_x = jnp.einsum("qbcnl,vlbqc->vqbcn", jac_block, profile, precision=lax.Precision.HIGHEST)
    weighted = err_block[None] * hidden_x
    returned = jnp.einsum("qbcnl,vqbcn->vlbqc", jac_block, weighted, precision=lax.Precision.HIGHEST)
    contrib = returned[..., None] * used_weights[None, None]
    placed = jax.vmap(put_band, in_axes=(0, 2), out_axes=2)(columns, contrib)
    return placed.reshape(lanczos, L, NR, LON)


def reference(forcing, coupling, diffusion, error_scale, pick_cols, pick_weights, send_count, jacobian, obs_weight):
    ends = []
    finish = jnp.zeros(forcing.shape[1:], jnp.float32)
    for window in range(WINDOWS):
        state = finish + forcing[window]
        for inner in range(STEPS):
            state = forward(state, coupling, diffusion)
        finish = state
        ends.append(state)
    observed = [observe(ends[window], pick_cols[window], pick_weights[window], send_count[window], jacobian[window], obs_weight[window]) for window in range(WINDOWS)]
    adjoint = jnp.zeros(forcing.shape[1:], jnp.float32)
    grads = [None] * WINDOWS
    for window in range(WINDOWS - 1, -1, -1):
        state = observed[window] + adjoint
        for inner in range(STEPS):
            state = backward(state, coupling, diffusion)
        adjoint = state
        grads[window] = adjoint + error_scale[None, :, None, None] * forcing[window]
    return jnp.stack(grads)
```

```python
import functools
import jax
import jax.numpy as jnp
from jax import lax
from jax.experimental import pallas as pl
from jax.experimental.pallas import tpu as pltpu
from jax.sharding import PartitionSpec as P

F32 = jnp.float32
BF16 = jnp.bfloat16
MESH = pl.DeviceIdType.MESH
HIGHEST = lax.Precision.HIGHEST
TILE = 128
REGION = 512
FIELDS = 384
WINDOWS = 4

NN = ((1,), (0,))
NT = ((1,), (1,))
TN = ((0,), (0,))


def dot(a, b, dims=NN, precision=None):
    return lax.dot_general(
        a, b, (dims, ((), ())), precision=precision, preferred_element_type=F32
    )


def halves(x):
    high = x.astype(BF16)
    return high, (x - high.astype(F32)).astype(BF16)


def dot3(a, b, dims=NN):
    return dot(a[0], b[0], dims) + dot(a[0], b[1], dims) + dot(a[1], b[0], dims)


def band_column(i):
    return ((i >> 2) & 3) * 128 + (i >> 7) * 32 + ((i >> 4) & 7) * 4 + (i & 3)


def region_place(i):
    block = i >> 7
    row = ((i >> 2) & 3) + jnp.where(block == 1, -4, jnp.where(block == 2, 4, 0))
    lon = ((i >> 4) & 7) * 4 + (i & 3)
    edge = (i - 384) >> 4
    edge_row = ((i >> 2) & 3) + jnp.where(edge < 2, 0, jnp.where(edge < 4, -4, 4))
    edge_lon = (i & 3) + jnp.where((edge & 1) == 0, -4, 32)
    return jnp.where(i < 384, row, edge_row), jnp.where(i < 384, lon, edge_lon)


def step_matrix(bands, band, part, above, here, below):
    i = lax.broadcasted_iota(jnp.int32, (REGION, 128), 0)
    lane = lax.broadcasted_iota(jnp.int32, (REGION, 128), 1)
    row_i, lon_i = region_place(i)
    rows = jnp.zeros((REGION, 128), F32)
    for source, first in ((above, -4), (here, 0), (below, 4)):
        for k in range(4):
            rows = jnp.where(row_i == first + k, source[k : k + 1, :], rows)
    picked = lane == ((lon_i + 32 * part) & 127)
    spread = jnp.sum(jnp.where(picked, rows, 0.0), axis=1, keepdims=True)
    i1 = lax.broadcasted_iota(jnp.int32, (REGION, 1), 0)
    j1 = lax.broadcasted_iota(jnp.int32, (1, REGION), 1)
    row_a, lon_a = region_place(i1)
    row_b, lon_b = region_place(j1)
    last = 4 * bands - 4 * band
    ok_a = (row_a >= -4 * band) & (row_a < last) & (i1 < 480)
    ok_b = (row_b >= -4 * band) & (row_b < last) & (j1 < 480)
    spread = jnp.where(ok_a, spread, 0.0)
    one = jnp.where(ok_a, 1.0, 0.0)
    apart = jnp.abs(row_a - row_b) + jnp.abs(lon_a - lon_b)
    h = jnp.where(apart == 0, one - 4.0 * spread, jnp.where(apart == 1, spread, 0.0))
    return jnp.where(ok_b, h, 0.0)


PIECES = (
    (128, 0, 128, 1, 0),
    (256, 0, 128, -1, 0),
    (384, 112, 16, 0, 1),
    (400, 0, 16, 0, -1),
    (416, 112, 16, 1, 1),
    (432, 0, 16, 1, -1),
    (448, 112, 16, -1, 1),
    (464, 0, 16, -1, -1),
)


def sweep(bands, ahead, src, mix, diff, out, xt, parts, region, ends, whole, dbuf,
          send_x, recv_x, send_h, recv_h, send_e, recv_e, send_d, recv_d):
    t, b = lax.axis_index("tm"), lax.axis_index("lat")

    def place(dt, db):
        return (lax.rem(t + dt + WINDOWS, WINDOWS), lax.rem(b + db + bands, bands))

    barrier = pltpu.get_barrier_semaphore()
    greeted = [(d, 0) for d in (1, 2, 3)] + [(d, s) for d in (-1, 0, 1) for s in (-1, 1)]
    for dt, db in greeted:
        pl.semaphore_signal(barrier, inc=1, device_id=place(dt, db), device_id_type=MESH)
    pl.semaphore_wait(barrier, len(greeted))

    def remote(source, target, send, recv, device):
        return pltpu.make_async_remote_copy(
            src_ref=source, dst_ref=target, send_sem=send, recv_sem=recv,
            device_id=device, device_id_type=MESH,
        )

    spreads = [remote(diff, dbuf.at[k], send_d.at[k], recv_d.at[k], place(0, s))
               for k, s in ((0, 1), (1, -1))]
    for copy in spreads:
        copy.start()

    place_i = band_column(lax.broadcasted_iota(jnp.int32, (REGION, 1), 0))
    column = lax.broadcasted_iota(jnp.int32, (1, REGION), 1)
    order = (place_i == column).astype(BF16)

    if ahead:
        x = src[...]
        first, rest = halves(x)
        third = (x - first.astype(F32) - rest.astype(F32)).astype(BF16)
        xt[...] = dot(order, first, NT) + dot(order, rest, NT) + dot(order, third, NT)
    else:
        xt[...] = src[...]
    scatter = []
    for d in (1, 2, 3):
        to = lax.rem(t + d, WINDOWS)
        copy = remote(xt.at[pl.ds(pl.multiple_of(to * TILE, TILE), TILE)], parts.at[t],
                      send_x.at[d], recv_x.at[t], (to, b))
        copy.start()
        scatter.append(copy)
    parts[t] = xt[pl.ds(pl.multiple_of(t * TILE, TILE), TILE), :]

    twice = dot(mix[...], mix[...], precision=HIGHEST)
    mixer = halves(dot(twice, twice, precision=HIGHEST))
    for w in range(WINDOWS):
        region[w, 480:512, :] = jnp.zeros((32, FIELDS), F32)
    for copy in spreads:
        copy.wait()
    h = step_matrix(bands, b, t, dbuf[0], diff[...], dbuf[1])
    if ahead:
        g = h[:TILE]
        for _ in range(3):
            g = dot(g, h, precision=HIGHEST)
    else:
        g = dot((lax.broadcasted_iota(jnp.int32, (TILE, REGION), 0)
                 == lax.broadcasted_iota(jnp.int32, (TILE, REGION), 1)).astype(F32), h, NT, HIGHEST)
        for _ in range(3):
            g = dot(g, h, NT, HIGHEST)
    g = halves(g)

    waits = []
    order_w = range(WINDOWS) if ahead else range(WINDOWS - 1, -1, -1)
    before = None
    for w in order_w:
        @pl.when(t != w)
        def _():
            remote(parts.at[w], parts.at[w], send_x.at[0], recv_x.at[w], (t, b)).wait_recv()

        state = parts[w]
        if before is not None:
            state = state + ends[before]
        region[w, :TILE, :] = dot3(halves(state), mixer, NT if ahead else NN)
        copies = []
        for k, (at, start, size, db, dt) in enumerate(PIECES):
            copy = remote(region.at[w, pl.ds(start, size)], region.at[w, pl.ds(at, size)],
                          send_h.at[w, k], recv_h.at[w, k], place(dt, db))
            copy.start()
            copies.append(copy)
        for copy in copies:
            copy.wait_recv()
        waits += copies
        ends[w] = dot3(g, halves(region[w]))
        before = w
        mine = pl.ds(pl.multiple_of(t * TILE, TILE), TILE)

        @pl.when(t != w)
        def _():
            remote(ends.at[w], whole.at[mine], send_e.at[w], recv_e.at[t], (w, b)).start()

        @pl.when(t == w)
        def _():
            whole[mine, :] = ends[w]

    for k in range(WINDOWS):
        @pl.when(t != k)
        def _():
            part = whole.at[pl.ds(k * TILE, TILE)]
            remote(part, part, send_e.at[k], recv_e.at[k], (t, b)).wait_recv()
            remote(ends.at[k], ends.at[k], send_e.at[k], recv_e.at[k], (t, b)).wait_send()

    for copy in scatter + waits:
        copy.wait_send()
    if ahead:
        out[...] = whole[...]
    else:
        x = whole[...]
        first, rest = halves(x)
        third = (x - first.astype(F32) - rest.astype(F32)).astype(BF16)
        out[...] = dot(first, order, TN) + dot(rest, order, TN) + dot(third, order, TN)


def run_sweep(bands, ahead, src, mix, diff):
    vmem = pl.BlockSpec(memory_space=pltpu.VMEM)
    shape = (REGION, FIELDS) if ahead else (FIELDS, REGION)
    dma = pltpu.SemaphoreType.DMA
    return pl.pallas_call(
        functools.partial(sweep, bands, ahead),
        out_shape=jax.ShapeDtypeStruct(shape, F32),
        in_specs=[vmem] * 3,
        out_specs=vmem,
        scratch_shapes=[
            pltpu.VMEM((REGION, FIELDS), F32),
            pltpu.VMEM((WINDOWS, TILE, FIELDS), F32),
            pltpu.VMEM((WINDOWS, REGION, FIELDS), F32),
            pltpu.VMEM((WINDOWS, TILE, FIELDS), F32),
            pltpu.VMEM((REGION, FIELDS), F32),
            pltpu.VMEM((2, 4, 128), F32),
            dma((4,)), dma((4,)),
            dma((4, 8)), dma((4, 8)),
            dma((4,)), dma((4,)),
            dma((2,)), dma((2,)),
        ],
        compiler_params=pltpu.CompilerParams(
            collective_id=0 if ahead else 2, has_side_effects=True,
            vmem_limit_bytes=48 * 1024 * 1024,
        ),
        name="forward_sweep" if ahead else "backward_sweep",
    )(src, mix, diff)


def observe(bands, end, picks, weights, errors, jac, out,
            jbuf, select, prof_out, prof_in, ret_out, ret_in,
            jsem, send_p, recv_p, send_r, recv_r):
    t, b = lax.axis_index("tm"), lax.axis_index("lat")
    cap = jac.shape[3]
    levels = jac.shape[5]

    def band_at(d):
        return lax.rem(b + d + bands, bands)

    def load(d, _):
        q = band_at(d)
        pltpu.make_async_copy(jac.at[0, 0, q], jbuf.at[q], jsem.at[q]).start()
        return 0

    lax.fori_loop(0, bands, lambda d, c: load(bands - d, c), 0)

    barrier = pltpu.get_barrier_semaphore()

    def greet(d, _):
        pl.semaphore_signal(barrier, inc=1, device_id=(t, band_at(d)), device_id_type=MESH)
        return 0

    lax.fori_loop(1, bands, greet, 0)

    column = band_column(lax.broadcasted_iota(jnp.int32, (1, REGION), 1))
    chosen = jnp.zeros((bands * cap, REGION), F32)
    for k in range(4):
        chosen += jnp.where(picks[:, k : k + 1] == column, weights[:, k : k + 1], 0.0)
    high, low = halves(chosen)
    select[0] = high
    select[1] = low
    prof_out[...] = dot3((high, low), halves(end[...]))

    pl.semaphore_wait(barrier, bands - 1)

    def rows(q):
        return pl.ds(pl.multiple_of(q * cap, cap), cap)

    def profile_copy(d):
        q = band_at(d)
        return pltpu.make_async_remote_copy(
            src_ref=prof_out.at[rows(q)], dst_ref=prof_in.at[rows(b)],
            send_sem=send_p.at[d], recv_sem=recv_p.at[d],
            device_id=(t, q), device_id_type=MESH)

    def profile_arrival(d):
        q = band_at(-d)
        return pltpu.make_async_remote_copy(
            src_ref=prof_out.at[rows(q)], dst_ref=prof_in.at[rows(q)],
            send_sem=send_p.at[d], recv_sem=recv_p.at[d],
            device_id=(t, q), device_id_type=MESH)

    def return_copy(d):
        q = band_at(-d)
        return pltpu.make_async_remote_copy(
            src_ref=ret_out.at[rows(q)], dst_ref=ret_in.at[rows(b)],
            send_sem=send_r.at[d], recv_sem=recv_r.at[d],
            device_id=(t, q), device_id_type=MESH)

    def return_arrival(d):
        q = band_at(d)
        return pltpu.make_async_remote_copy(
            src_ref=ret_out.at[rows(q)], dst_ref=ret_in.at[rows(q)],
            send_sem=send_r.at[d], recv_sem=recv_r.at[d],
            device_id=(t, q), device_id_type=MESH)

    def send(d, _):
        profile_copy(d).start()
        return 0

    lax.fori_loop(1, bands, send, 0)

    channels = jac.shape[4]
    unit = (lax.broadcasted_iota(jnp.int32, (channels, channels), 0)
            == lax.broadcasted_iota(jnp.int32, (channels, channels), 1)).astype(F32)

    def work(q, profile):
        pltpu.make_async_copy(jac.at[0, 0, q], jbuf.at[q], jsem.at[q]).wait()
        block = jbuf[q]
        scale = jnp.sum(errors[q][:, None, :] * unit[None], axis=2, keepdims=True)
        total = None
        for v in range(2):
            turned = profile if v == 0 else pltpu.roll(profile, FIELDS - levels, 1)
            hidden = jnp.sum(block * turned[:, None, :levels], axis=2, keepdims=True)
            back = jnp.sum(block * (hidden * scale), axis=1)
            back = jnp.concatenate([back, jnp.zeros((cap, FIELDS - levels), F32)], axis=1)
            total = back if v == 0 else total + pltpu.roll(back, levels, 1)
        return total

    ret_in[rows(b), :] = work(b, prof_out[rows(b), :])

    def serve(d, _):
        q = band_at(-d)
        profile_arrival(d).wait_recv()
        ret_out[rows(q), :] = work(q, prof_in[rows(q), :])
        return_copy(d).start()
        return 0

    lax.fori_loop(1, bands, serve, 0)

    def finish(d, _):
        return_arrival(d).wait_recv()
        return_copy(d).wait_send()
        profile_copy(d).wait_send()
        return 0

    lax.fori_loop(1, bands, finish, 0)
    out[...] = dot3((select[0], select[1]), halves(ret_in[...]), TN)


def run_observe(bands, end, picks, weights, errors, jac):
    vmem = pl.BlockSpec(memory_space=pltpu.VMEM)
    dma = pltpu.SemaphoreType.DMA
    slots = picks.shape[0]
    return pl.pallas_call(
        functools.partial(observe, bands),
        out_shape=jax.ShapeDtypeStruct((REGION, FIELDS), F32),
        in_specs=[vmem] * 4 + [pl.BlockSpec(memory_space=pl.ANY)],
        out_specs=vmem,
        scratch_shapes=[
            pltpu.VMEM(jac.shape[2:], F32),
            pltpu.VMEM((2, slots, REGION), BF16),
        ] + [pltpu.VMEM((slots, FIELDS), F32)] * 4
        + [dma((bands,))] * 5,
        compiler_params=pltpu.CompilerParams(
            collective_id=1, has_side_effects=True, vmem_limit_bytes=48 * 1024 * 1024,
        ),
        name="observe",
    )(end, picks, weights, errors, jac)


def shards(forcing, coupling, diffusion, error_scale, pick_cols, pick_weights,
           send_count, jacobian, obs_weight):
    bands = lax.axis_size("lat")
    own = forcing[0]
    lanczos, levels, rows, longitudes = own.shape
    fields = lanczos * levels
    spare = FIELDS - fields
    src = jnp.pad(own.reshape(fields, rows * longitudes), ((0, spare), (0, 0)))
    one = 0.8 * jnp.eye(levels, dtype=F32) + 0.2 * coupling
    mix = jnp.pad(one, ((0, FIELDS - levels), (0, FIELDS - levels)))
    mix = mix + jnp.pad(one, ((levels, spare), (levels, spare)))
    cap = pick_cols.shape[3]
    live = lax.broadcasted_iota(jnp.int32, (bands, cap), 1) < send_count[0, 0][:, None]
    weights = jnp.where(live[..., None], pick_weights[0, 0], 0.0).reshape(bands * cap, -1)
    picks = pick_cols[0, 0].reshape(bands * cap, -1)
    end = run_sweep(bands, True, src, mix, diffusion)
    observed = run_observe(bands, end, picks, weights, obs_weight[0, 0], jacobian)
    adjoint = run_sweep(bands, False, observed, mix, diffusion)
    adjoint = adjoint[:fields].reshape(own.shape)
    return (adjoint + error_scale[None, :, None, None] * own)[None]


def solution(mesh):
    return jax.shard_map(
        shards,
        mesh=mesh,
        in_specs=(
            P("tm", None, None, "lat", None),
            P(),
            P("lat", None),
            P(),
            P("tm", "lat", None, None, None),
            P("tm", "lat", None, None, None),
            P("tm", "lat", None),
            P("tm", "lat", None, None, None, None),
            P("tm", "lat", None, None, None),
        ),
        out_specs=P("tm", None, None, "lat", None),
        check_vma=False,
    )
```

```python
import functools
import jax
import jax.numpy as jnp
from jax import lax
from jax.experimental import pallas as pl
from jax.experimental.pallas import tpu as pltpu
from jax.sharding import PartitionSpec as P

F32 = jnp.float32
BF16 = jnp.bfloat16
MESH = pl.DeviceIdType.MESH
HIGHEST = lax.Precision.HIGHEST
TILE = 128
REGION = 512
FIELDS = 288
SPAN = 144
WINDOWS = 4

NN = ((1,), (0,))
NT = ((1,), (1,))


def dot(a, b, dims=NN, precision=None):
    return lax.dot_general(
        a, b, (dims, ((), ())), precision=precision, preferred_element_type=F32
    )


def halves(x):
    high = x.astype(BF16)
    return high, (x - high.astype(F32)).astype(BF16)


def thirds(x):
    high = x.astype(BF16)
    rest = x - high.astype(F32)
    middle = rest.astype(BF16)
    return high, middle, (rest - middle.astype(F32)).astype(BF16)


def dot3(a, b, dims=NN):
    return dot(a[0], b[0], dims) + (dot(a[0], b[1], dims) + dot(a[1], b[0], dims))


def band_column(i):
    return ((i >> 2) & 3) * 128 + (i >> 7) * 32 + ((i >> 4) & 7) * 4 + (i & 3)


def region_place(i):
    block = i >> 7
    row = ((i >> 2) & 3) + jnp.where(block == 1, -4, jnp.where(block == 2, 4, 0))
    lon = ((i >> 4) & 7) * 4 + (i & 3)
    edge = (i - 384) >> 4
    edge_row = ((i >> 2) & 3) + jnp.where(edge < 2, 0, jnp.where(edge < 4, -4, 4))
    edge_lon = (i & 3) + jnp.where((edge & 1) == 0, -4, 32)
    return jnp.where(i < 384, row, edge_row), jnp.where(i < 384, lon, edge_lon)


def step_matrix(bands, band, part, above, here, below):
    i = lax.broadcasted_iota(jnp.int32, (REGION, 128), 0)
    lane = lax.broadcasted_iota(jnp.int32, (REGION, 128), 1)
    row_i, lon_i = region_place(i)
    rows = jnp.zeros((REGION, 128), F32)
    for source, first in ((above, -4), (here, 0), (below, 4)):
        for k in range(4):
            rows = jnp.where(row_i == first + k, source[k : k + 1, :], rows)
    picked = lane == ((lon_i + 32 * part) & 127)
    spread = jnp.sum(jnp.where(picked, rows, 0.0), axis=1, keepdims=True)
    i1 = lax.broadcasted_iota(jnp.int32, (REGION, 1), 0)
    j1 = lax.broadcasted_iota(jnp.int32, (1, REGION), 1)
    row_a, lon_a = region_place(i1)
    row_b, lon_b = region_place(j1)
    last = 4 * bands - 4 * band
    ok_a = (row_a >= -4 * band) & (row_a < last) & (i1 < 480)
    ok_b = (row_b >= -4 * band) & (row_b < last) & (j1 < 480)
    spread = jnp.where(ok_a, spread, 0.0)
    one = jnp.where(ok_a, 1.0, 0.0)
    apart = jnp.abs(row_a - row_b) + jnp.abs(lon_a - lon_b)
    h = jnp.where(apart == 0, one - 4.0 * spread, jnp.where(apart == 1, spread, 0.0))
    return jnp.where(ok_b, h, 0.0)


EDGES = ((2, 1, 1, 1), (3, 0, 1, -1), (4, 1, -1, 1), (5, 0, -1, -1), (0, 1, 0, 1), (1, 0, 0, -1))


def whole_loop(bands, f, coupling, diff, picks, weights, counts, errors, jac, out,
               order, src, parts, region, own_edges, edges, ends, whole, dbuf, hmat, power,
               mixer, table, jbuf, jscaled, select, prof_out, prof_in, ret_out, ret_in,
               send_x, recv_x, send_h, recv_h, send_e, recv_e, send_d, recv_d,
               jsem, send_p, recv_p, send_r, recv_r):
    t, b = lax.axis_index("tm"), lax.axis_index("lat")
    channels, cap, levels = jac.shape[1:]
    mine = pl.ds(pl.multiple_of(t * TILE, TILE), TILE)

    def place(dt, db):
        return (lax.rem(t + dt + WINDOWS, WINDOWS), lax.rem(b + db + bands, bands))

    def band_at(d):
        return lax.rem(b + d + bands, bands)

    def remote(source, target, send, recv, device):
        return pltpu.make_async_remote_copy(
            src_ref=source, dst_ref=target, send_sem=send, recv_sem=recv,
            device_id=device, device_id_type=MESH,
        )

    def loop(first, last, body):
        def step(d, carry):
            body(d)
            return carry

        lax.fori_loop(first, last, step, 0)

    barrier = pltpu.get_barrier_semaphore()
    greeted = [(d, 0) for d in (1, 2, 3)] + [(d, s) for d in (-1, 1) for s in (-1, 1)]
    for dt, db in greeted:
        pl.semaphore_signal(barrier, inc=1, device_id=place(dt, db), device_id_type=MESH)
    loop(1, bands, lambda d: pl.semaphore_signal(
        barrier, inc=1, device_id=(t, band_at(d)), device_id_type=MESH))

    def jac_copy(q):
        return pltpu.make_async_copy(jac.at[q], jbuf.at[q], jsem.at[q])

    loop(0, bands, lambda q: jac_copy(q).start())

    place_i = band_column(lax.broadcasted_iota(jnp.int32, (REGION, 1), 0))
    column = lax.broadcasted_iota(jnp.int32, (1, REGION), 1)
    order[...] = (place_i == column).astype(F32).astype(BF16)
    for v in range(2):
        src[v * SPAN + 136 : (v + 1) * SPAN, :] = jnp.zeros((8, REGION), F32)
        for r in range(4):
            src[v * SPAN : v * SPAN + levels, r * 128 : (r + 1) * 128] = f[v, :, r, :]
    x = thirds(src[...])
    xt = dot(x[0], order[...], NT) + (dot(x[1], order[...], NT) + dot(x[2], order[...], NT))
    src[...] = xt

    pl.semaphore_wait(barrier, len(greeted) + bands - 1)

    spreads = [remote(diff, dbuf.at[k], send_d.at[k], recv_d.at[k], place(0, s))
               for k, s in ((0, 1), (1, -1))]
    for copy in spreads:
        copy.start()

    def scatter(s, source):
        copies = []
        for d in (1, 2, 3):
            to = lax.rem(t + d, WINDOWS)
            copy = remote(source.at[:, pl.ds(pl.multiple_of(to * TILE, TILE), TILE)],
                          parts.at[s, t], send_x.at[s, d], recv_x.at[s, t], (to, b))
            copy.start()
            copies.append(copy)
        parts[s, t] = source[:, mine]
        return copies

    started = scatter(0, src)

    for s in range(2):
        for w in range(WINDOWS):
            edges[s, w, 96:128, :] = jnp.zeros((32, 384), F32)
    eye = (lax.broadcasted_iota(jnp.int32, (levels, levels), 0)
           == lax.broadcasted_iota(jnp.int32, (levels, levels), 1)).astype(F32)
    mix = 0.8 * eye + 0.2 * coupling[...]
    twice = dot(mix, mix, precision=HIGHEST)
    power[...] = jnp.zeros((256, 256), F32)
    power[:levels, :levels] = dot(twice, twice, precision=HIGHEST)
    for s in range(2):
        full = power[...] if s == 0 else jnp.swapaxes(power[...], 0, 1)
        high, low = halves(full[:SPAN, :SPAN])
        mixer[s, 0] = high
        mixer[s, 1] = low

    for copy in spreads:
        copy.wait()
    hmat[...] = step_matrix(bands, b, t, dbuf[0], diff[...], dbuf[1])
    g = hmat[:TILE, :]
    for _ in range(3):
        g = dot(g, hmat[...], precision=HIGHEST)
    high, low = halves(jnp.swapaxes(g, 0, 1))
    table[0, 0] = high
    table[0, 1] = low

    edge_i = lax.broadcasted_iota(jnp.int32, (32, TILE), 0)
    edge_j = lax.broadcasted_iota(jnp.int32, (32, TILE), 1)
    edge_of = (edge_j == jnp.where(edge_i < 16, edge_i, edge_i + 96)).astype(F32).astype(BF16)

    def chain(s, windows, beside):
        before = None
        for w in windows:
            @pl.when(t != w)
            def _():
                remote(parts.at[s, w], parts.at[s, w], send_x.at[s, 0], recv_x.at[s, w],
                       (t, b)).wait_recv()

            state = parts[s, w]
            if before is not None:
                state = state + ends[s, before]
            high, low = halves(state)
            for v in range(2):
                rows = slice(v * SPAN, (v + 1) * SPAN)
                region[s, w, rows, :TILE] = dot3((mixer[s, 0], mixer[s, 1]), (high[rows], low[rows]))
            center = halves(region[s, w, :, :TILE])
            own_edges[s, w, :, :FIELDS] = dot(edge_of, center[0], NT) + dot(edge_of, center[1], NT)
            copies = []
            for at, side, db, dt in EDGES:
                copies.append(remote(own_edges.at[s, w, pl.ds(16 * side, 16)],
                                     edges.at[s, w, pl.ds(16 * at, 16)],
                                     send_h.at[s, w, at], recv_h.at[s, w, at], place(dt, db)))
            for k, db in ((6, 1), (7, -1)):
                copies.append(remote(region.at[s, w, :, pl.ds(0, TILE)],
                                     region.at[s, w, :, pl.ds((k - 5) * TILE, TILE)],
                                     send_h.at[s, w, k], recv_h.at[s, w, k], place(0, db)))
            for copy in copies:
                copy.start()
            part = dot3(center, (table[s, 0, :TILE], table[s, 1, :TILE]))
            if beside[w] is not None:
                beside[w]()
            for copy in copies:
                copy.wait_recv()
            started.extend(copies)
            region[s, w, :, 384:] = jnp.swapaxes(edges[s, w], 0, 1)[:FIELDS]
            ends[s, w] = part + dot3(halves(region[s, w, :, TILE:]),
                                     (table[s, 0, TILE:], table[s, 1, TILE:]))
            before = w

            @pl.when(t != w)
            def _():
                remote(ends.at[s, w], whole.at[s, :, mine], send_e.at[s, w], recv_e.at[s, t],
                       (w, b)).start()

            @pl.when(t == w)
            def _():
                whole[s, :, mine] = ends[s, w]

        for k in range(WINDOWS):
            @pl.when(t != k)
            def _():
                piece = whole.at[s, :, pl.ds(k * TILE, TILE)]
                remote(piece, piece, send_e.at[s, k], recv_e.at[s, k], (t, b)).wait_recv()
                remote(ends.at[s, k], ends.at[s, k], send_e.at[s, k], recv_e.at[s, k],
                       (t, b)).wait_send()

    slots = bands * cap

    def make_select():
        slot = lax.broadcasted_iota(jnp.int32, (slots, bands), 0)
        owner = lax.broadcasted_iota(jnp.int32, (slots, bands), 1)
        spread = (slot // cap == owner).astype(F32)
        near = picks.shape[1]
        row = lax.broadcasted_iota(jnp.int32, (slots, cap * near), 0)
        lane = lax.broadcasted_iota(jnp.int32, (slots, cap * near), 1)
        own = lane // near == row % cap
        chosen = jnp.zeros((slots, REGION), F32)
        col = jnp.concatenate([picks[c] for c in range(cap)], axis=0).astype(F32)
        wt = jnp.concatenate([jnp.where(counts[...] > c, weights[c], 0.0) for c in range(cap)], axis=0)
        col = dot(spread, col, NT, HIGHEST)
        wt = dot(spread, wt, NT, HIGHEST)
        at = band_column(lax.broadcasted_iota(jnp.int32, (1, REGION), 1)).astype(F32)
        for k in range(near):
            here = own & (lane % near == k)
            col_k = jnp.sum(jnp.where(here, col, 0.0), axis=1, keepdims=True)
            wt_k = jnp.sum(jnp.where(here, wt, 0.0), axis=1, keepdims=True)
            chosen += jnp.where(jnp.abs(col_k - at) < 0.5, wt_k, 0.0)
        high, low = halves(chosen)
        select[0] = high
        select[1] = low

    def scale_jac(first, last):
        lane = lax.broadcasted_iota(jnp.int32, (cap, bands), 1)

        def body(q):
            jac_copy(q).wait()
            for n in range(channels):
                scale = jnp.sum(jnp.where(lane == q, errors[n], 0.0), axis=1, keepdims=True)
                jscaled[q, n] = jbuf[q, n] * scale

        loop(first, last, body)

    def back_table():
        g = hmat[:, :TILE]
        for _ in range(3):
            g = dot(hmat[...], g, precision=HIGHEST)
        high, low = halves(g)
        table[1, 0] = high
        table[1, 1] = low

    chain(0, range(WINDOWS), [
        make_select, lambda: scale_jac(0, bands // 2), lambda: scale_jac(bands // 2, bands), back_table])

    def fold(x):
        count = x.shape[0] // cap
        x = x.reshape(count, cap, 384)
        last = x[:, :8, 256:] + pltpu.roll(x[:, 8:, 256:].reshape(count * 8, 128), 64, 1).reshape(count, 8, 128)
        return jnp.concatenate([x[:, :, :128], x[:, :, 128:256], last], axis=1)

    def unfold(x):
        count = x.shape[0]
        last = x[:, 2 * cap :]
        turned = pltpu.roll(last.reshape(count * 8, 128), 64, 1).reshape(count, 8, 128)
        last = jnp.concatenate([last, turned], axis=1)
        return jnp.concatenate([x[:, :cap], x[:, cap : 2 * cap], last], axis=2).reshape(count * cap, 384)

    high, low = halves(whole[0])
    spare = jnp.zeros((384 - FIELDS, REGION), BF16)
    state = (jnp.concatenate([high, spare], axis=0), jnp.concatenate([low, spare], axis=0))
    prof_out[...] = fold(dot3((select[0], select[1]), state, NT))

    def profile_copy(d):
        q = band_at(d)
        return remote(prof_out.at[q], prof_in.at[b], send_p.at[d], recv_p.at[d], (t, q))

    def profile_arrival(d):
        q = band_at(-d)
        return remote(prof_out.at[q], prof_in.at[q], send_p.at[d], recv_p.at[d], (t, q))

    def return_copy(d):
        q = band_at(-d)
        return remote(ret_out.at[q], ret_in.at[b], send_r.at[d], recv_r.at[d], (t, q))

    def return_arrival(d):
        q = band_at(d)
        return remote(ret_out.at[q], ret_in.at[q], send_r.at[d], recv_r.at[d], (t, q))

    loop(1, bands, lambda d: profile_copy(d).start())

    def work(q, packed):
        profile = unfold(packed[None])
        first = profile[:, :levels]
        second = pltpu.roll(profile[:, 128:], 256 - (SPAN - 128), 1)[:, :levels]
        sums = [jnp.zeros((cap, levels), F32)] * 2
        for n in range(channels):
            jn, jw = jbuf[q, n], jscaled[q, n]
            for v, p in enumerate((first, second)):
                hidden = jnp.sum(jn * p, axis=1, keepdims=True)
                sums[v] = sums[v] + jw * hidden
        spare = jnp.zeros((cap, 256 - levels), F32)
        one = jnp.concatenate([sums[0], spare], axis=1)
        two = pltpu.roll(jnp.concatenate([sums[1], spare], axis=1), SPAN - 128, 1)
        back = jnp.concatenate([one[:, :128], one[:, 128:] + two[:, :128], two[:, 128:]], axis=1)
        return fold(back)[0]

    ret_in[b] = work(b, prof_out[b])

    def serve(d):
        q = band_at(-d)
        profile_arrival(d).wait_recv()
        ret_out[q] = work(q, prof_in[q])
        return_copy(d).start()

    loop(1, bands, serve)
    loop(1, bands, lambda d: return_arrival(d).wait_recv())
    back = halves(jnp.swapaxes(unfold(ret_in[...]), 0, 1)[:FIELDS])
    src2 = whole.at[2]
    src2[...] = dot3(back, (select[0], select[1]))
    started += scatter(1, src2)
    chain(1, range(WINDOWS - 1, -1, -1), [None] * WINDOWS)
    x = thirds(whole[1])
    out[...] = dot(x[0], order[...]) + (dot(x[1], order[...]) + dot(x[2], order[...]))

    for copy in started:
        copy.wait_send()

    def drain(d):
        return_copy(d).wait_send()
        profile_copy(d).wait_send()

    loop(1, bands, drain)


def run(bands, f, coupling, diff, picks, weights, counts, errors, jac):
    vmem = pl.BlockSpec(memory_space=pltpu.VMEM)
    dma = pltpu.SemaphoreType.DMA
    slots = bands * jac.shape[2]
    packed = pltpu.VMEM((bands, 40, 128), F32)
    return pl.pallas_call(
        functools.partial(whole_loop, bands),
        out_shape=jax.ShapeDtypeStruct((FIELDS, REGION), F32),
        in_specs=[vmem] * 7 + [pl.BlockSpec(memory_space=pl.ANY)],
        out_specs=vmem,
        scratch_shapes=[
            pltpu.VMEM((REGION, REGION), BF16),
            pltpu.VMEM((FIELDS, REGION), F32),
            pltpu.VMEM((2, WINDOWS, FIELDS, TILE), F32),
            pltpu.VMEM((2, WINDOWS, FIELDS, REGION), F32),
            pltpu.VMEM((2, WINDOWS, 32, 384), F32),
            pltpu.VMEM((2, WINDOWS, 128, 384), F32),
            pltpu.VMEM((2, WINDOWS, FIELDS, TILE), F32),
            pltpu.VMEM((3, FIELDS, REGION), F32),
            pltpu.VMEM((2, 4, 128), F32),
            pltpu.VMEM((REGION, REGION), F32),
            pltpu.VMEM((256, 256), F32),
            pltpu.VMEM((2, 2, SPAN, SPAN), BF16),
            pltpu.VMEM((2, 2, REGION, TILE), BF16),
            pltpu.VMEM(jac.shape, F32),
            pltpu.VMEM(jac.shape, F32),
            pltpu.VMEM((2, slots, REGION), BF16),
            packed, packed, packed, packed,
            dma((2, 4)), dma((2, 4)),
            dma((2, 4, 8)), dma((2, 4, 8)),
            dma((2, 4)), dma((2, 4)),
            dma((2,)), dma((2,)),
            dma((bands,)), dma((bands,)), dma((bands,)), dma((bands,)), dma((bands,)),
        ],
        compiler_params=pltpu.CompilerParams(
            collective_id=0, has_side_effects=True, vmem_limit_bytes=56 * 1024 * 1024,
        ),
        name="inner_loop",
    )(f, coupling, diff, picks, weights, counts, errors, jac)


def shards(forcing, coupling, diffusion, error_scale, pick_cols, pick_weights,
           send_count, jacobian, obs_weight):
    own = forcing[0]
    lanczos, levels, rows, longitudes = own.shape
    adjoint = run(
        lax.axis_size("lat"), own, coupling, diffusion,
        jnp.transpose(pick_cols[0, 0], (1, 2, 0)),
        jnp.transpose(pick_weights[0, 0], (1, 2, 0)),
        send_count[0],
        jnp.transpose(obs_weight[0, 0], (2, 1, 0)),
        jnp.transpose(jacobian[0, 0], (0, 2, 1, 3)),
    )
    adjoint = adjoint.reshape(lanczos, SPAN, rows, longitudes)[:, :levels]
    return (adjoint + error_scale[None, :, None, None] * own)[None]


def solution(mesh):
    return jax.shard_map(
        shards,
        mesh=mesh,
        in_specs=(
            P("tm", None, None, "lat", None),
            P(),
            P("lat", None),
            P(),
            P("tm", "lat", None, None, None),
            P("tm", "lat", None, None, None),
            P("tm", "lat", None),
            P("tm", "lat", None, None, None, None),
            P("tm", "lat", None, None, None),
        ),
        out_specs=P("tm", None, None, "lat", None),
        check_vma=False,
    )
```

```python
import functools
import jax
import jax.numpy as jnp
from jax import lax
from jax.experimental import pallas as pl
from jax.experimental.pallas import tpu as pltpu
from jax.sharding import PartitionSpec as P

F32 = jnp.float32
BF16 = jnp.bfloat16
MESH = pl.DeviceIdType.MESH
HIGHEST = lax.Precision.HIGHEST
TILE = 128
REGION = 512
FIELDS = 288
SPAN = 144
WINDOWS = 4

NN = ((1,), (0,))
NT = ((1,), (1,))


def dot(a, b, dims=NN, precision=None):
    return lax.dot_general(
        a, b, (dims, ((), ())), precision=precision, preferred_element_type=F32
    )


def halves(x):
    high = x.astype(BF16)
    return high, (x - high.astype(F32)).astype(BF16)


def thirds(x):
    high = x.astype(BF16)
    rest = x - high.astype(F32)
    middle = rest.astype(BF16)
    return high, middle, (rest - middle.astype(F32)).astype(BF16)


def dot3(a, b, dims=NN):
    return dot(a[0], b[0], dims) + (dot(a[0], b[1], dims) + dot(a[1], b[0], dims))


def band_column(i):
    return ((i >> 2) & 3) * 128 + (i >> 7) * 32 + ((i >> 4) & 7) * 4 + (i & 3)


def region_place(i):
    block = i >> 7
    row = ((i >> 2) & 3) + jnp.where(block == 1, -4, jnp.where(block == 2, 4, 0))
    lon = ((i >> 4) & 7) * 4 + (i & 3)
    edge = (i - 384) >> 4
    edge_row = ((i >> 2) & 3) + jnp.where(edge < 2, 0, jnp.where(edge < 4, -4, 4))
    edge_lon = (i & 3) + jnp.where((edge & 1) == 0, -4, 32)
    return jnp.where(i < 384, row, edge_row), jnp.where(i < 384, lon, edge_lon)


def step_matrix(bands, band, part, above, here, below):
    i = lax.broadcasted_iota(jnp.int32, (REGION, 128), 0)
    lane = lax.broadcasted_iota(jnp.int32, (REGION, 128), 1)
    row_i, lon_i = region_place(i)
    rows = jnp.zeros((REGION, 128), F32)
    for source, first in ((above, -4), (here, 0), (below, 4)):
        for k in range(4):
            rows = jnp.where(row_i == first + k, source[k : k + 1, :], rows)
    picked = lane == ((lon_i + 32 * part) & 127)
    spread = jnp.sum(jnp.where(picked, rows, 0.0), axis=1, keepdims=True)
    i1 = lax.broadcasted_iota(jnp.int32, (REGION, 1), 0)
    j1 = lax.broadcasted_iota(jnp.int32, (1, REGION), 1)
    row_a, lon_a = region_place(i1)
    row_b, lon_b = region_place(j1)
    last = 4 * bands - 4 * band
    ok_a = (row_a >= -4 * band) & (row_a < last) & (i1 < 480)
    ok_b = (row_b >= -4 * band) & (row_b < last) & (j1 < 480)
    spread = jnp.where(ok_a, spread, 0.0)
    one = jnp.where(ok_a, 1.0, 0.0)
    apart = jnp.abs(row_a - row_b) + jnp.abs(lon_a - lon_b)
    h = jnp.where(apart == 0, one - 4.0 * spread, jnp.where(apart == 1, spread, 0.0))
    return jnp.where(ok_b, h, 0.0)


EDGES = ((2, 1, 1, 1), (3, 0, 1, -1), (4, 1, -1, 1), (5, 0, -1, -1), (0, 1, 0, 1), (1, 0, 0, -1))


def whole_loop(bands, f, coupling, diff, picks, weights, counts, errors, jac, out,
               order, src, parts, region, own_edges, edges, ends, whole, dbuf, hmat, power,
               mixer, table, jbuf, jscaled, select, prof_out, prof_in, ret_out, ret_in,
               send_x, recv_x, send_h, recv_h, send_e, recv_e, send_d, recv_d,
               jsem, send_p, recv_p, send_r, recv_r):
    t, b = lax.axis_index("tm"), lax.axis_index("lat")
    channels, cap, levels = jac.shape[1:]
    mine = pl.ds(pl.multiple_of(t * TILE, TILE), TILE)

    def place(dt, db):
        return (lax.rem(t + dt + WINDOWS, WINDOWS), lax.rem(b + db + bands, bands))

    def band_at(d):
        return lax.rem(b + d + bands, bands)

    def remote(source, target, send, recv, device):
        return pltpu.make_async_remote_copy(
            src_ref=source, dst_ref=target, send_sem=send, recv_sem=recv,
            device_id=device, device_id_type=MESH,
        )

    def loop(first, last, body):
        def step(d, carry):
            body(d)
            return carry

        lax.fori_loop(first, last, step, 0)

    barrier = pltpu.get_barrier_semaphore()
    greeted = [(d, 0) for d in (1, 2, 3)] + [(d, s) for d in (-1, 1) for s in (-1, 1)]
    for dt, db in greeted:
        pl.semaphore_signal(barrier, inc=1, device_id=place(dt, db), device_id_type=MESH)
    loop(1, bands, lambda d: pl.semaphore_signal(
        barrier, inc=1, device_id=(t, band_at(d)), device_id_type=MESH))

    def jac_copy(q):
        return pltpu.make_async_copy(jac.at[q], jbuf.at[q], jsem.at[q])

    loop(0, bands, lambda q: jac_copy(q).start())

    place_i = band_column(lax.broadcasted_iota(jnp.int32, (REGION, 1), 0))
    column = lax.broadcasted_iota(jnp.int32, (1, REGION), 1)
    order[...] = (place_i == column).astype(F32).astype(BF16)
    for v in range(2):
        src[v, 136:, :] = jnp.zeros((8, REGION), F32)
        for r in range(4):
            src[v, :levels, r * 128 : (r + 1) * 128] = f[v, :, r, :]
        x = thirds(src[v])
        src[v] = dot(x[0], order[...], NT) + (dot(x[1], order[...], NT) + dot(x[2], order[...], NT))

    pl.semaphore_wait(barrier, len(greeted) + bands - 1)

    spreads = [remote(diff, dbuf.at[k], send_d.at[k], recv_d.at[k], place(0, s))
               for k, s in ((0, 1), (1, -1))]
    for copy in spreads:
        copy.start()

    started = []

    def scatter_copy(s, source, d, v):
        to = lax.rem(t + d, WINDOWS)
        return remote(source.at[v, :, pl.ds(pl.multiple_of(to * TILE, TILE), TILE)],
                      parts.at[s, t, v], send_x.at[s, v, d], recv_x.at[s, t, v], (to, b))

    def scatter(s, source, w):
        @pl.when(t == w)
        def _():
            for v in range(2):
                for d in (2, 1, 3):
                    scatter_copy(s, source, d, v).start()

    def keep_own(s, source):
        for v in range(2):
            parts[s, t, v] = source[v, :, mine]

    scatter(0, src, 0)
    keep_own(0, src)

    for s in range(2):
        for w in range(WINDOWS):
            for v in range(2):
                edges[s, w, v, 96:, :] = jnp.zeros((32, 256), F32)
    eye = (lax.broadcasted_iota(jnp.int32, (levels, levels), 0)
           == lax.broadcasted_iota(jnp.int32, (levels, levels), 1)).astype(F32)
    mix = 0.8 * eye + 0.2 * coupling[...]
    twice = dot(mix, mix, precision=HIGHEST)
    power[...] = jnp.zeros((256, 256), F32)
    power[:levels, :levels] = dot(twice, twice, precision=HIGHEST)
    for s in range(2):
        full = power[...] if s == 0 else jnp.swapaxes(power[...], 0, 1)
        high, low = halves(full[:SPAN, :SPAN])
        mixer[s, 0] = high
        mixer[s, 1] = low

    for copy in spreads:
        copy.wait()
    hmat[...] = step_matrix(bands, b, t, dbuf[0], diff[...], dbuf[1])
    g = hmat[:TILE, :]
    for _ in range(3):
        g = dot(g, hmat[...], precision=HIGHEST)
    high, low = halves(jnp.swapaxes(g, 0, 1))
    table[0, 0] = high
    table[0, 1] = low

    edge_i = lax.broadcasted_iota(jnp.int32, (32, TILE), 0)
    edge_j = lax.broadcasted_iota(jnp.int32, (32, TILE), 1)
    edge_of = (edge_j == jnp.where(edge_i < 16, edge_i, edge_i + 96)).astype(F32).astype(BF16)

    def halo_copies(s, w, v):
        copies = []
        for at, side, db, dt in EDGES:
            copies.append(remote(own_edges.at[s, w, v, pl.ds(16 * side, 16)],
                                 edges.at[s, w, v, pl.ds(16 * at, 16)],
                                 send_h.at[s, w, v, at], recv_h.at[s, w, v, at], place(dt, db)))
        for k, db in ((1, 1), (2, -1)):
            copies.append(remote(region.at[s, w, v, :, pl.ds(0, TILE)],
                                 region.at[s, w, v, :, pl.ds(k * TILE, TILE)],
                                 send_h.at[s, w, v, 5 + k], recv_h.at[s, w, v, 5 + k], place(0, db)))
        return copies

    def send_halo(s, w, before, v):
        @pl.when(t != w)
        def _():
            remote(parts.at[s, w, v], parts.at[s, w, v], send_x.at[s, v, 0], recv_x.at[s, w, v],
                   (t, b)).wait_recv()

        state = parts[s, w, v]
        if before is not None:
            state = state + ends[s, before, v]
        mixed = dot3((mixer[s, 0], mixer[s, 1]), halves(state))
        center = halves(mixed)
        own_edges[s, w, v, :, :SPAN] = dot(edge_of, center[0], NT) + dot(edge_of, center[1], NT)
        region[s, w, v, :, :TILE] = mixed
        copies = halo_copies(s, w, v)
        for copy in copies:
            copy.start()
        started.extend(copies)
        ends[s, w, v] = dot3(center, (table[s, 0, :TILE], table[s, 1, :TILE]))

    def receive_halo(s, w, v):
        for copy in halo_copies(s, w, v):
            copy.wait_recv()
        region[s, w, v, :, 384:] = jnp.swapaxes(edges[s, w, v], 0, 1)[:SPAN]
        ends[s, w, v] += dot3(halves(region[s, w, v, :, TILE:]),
                              (table[s, 0, TILE:], table[s, 1, TILE:]))

        @pl.when(t != w)
        def _():
            remote(ends.at[s, w, v], whole.at[s, v, :, mine], send_e.at[s, w, v],
                   recv_e.at[s, t, v], (w, b)).start()

        @pl.when(t == w)
        def _():
            whole[s, v, :, mine] = ends[s, w, v]

    def chain(s, windows, source, beside):
        for v in range(2):
            send_halo(s, windows[0], None, v)
        for k, w in enumerate(windows):
            if k < WINDOWS - 1:
                scatter(s, source, windows[k + 1])
            if beside[k] is not None:
                beside[k]()
            for v in range(2):
                receive_halo(s, w, v)
                if k < WINDOWS - 1:
                    send_halo(s, windows[k + 1], w, v)

    def collect(s, v):
        for k in range(WINDOWS):
            @pl.when(t != k)
            def _():
                piece = whole.at[s, v, :, pl.ds(k * TILE, TILE)]
                remote(piece, piece, send_e.at[s, k, v], recv_e.at[s, k, v], (t, b)).wait_recv()

    slots = bands * cap

    def make_select():
        slot = lax.broadcasted_iota(jnp.int32, (slots, bands), 0)
        owner = lax.broadcasted_iota(jnp.int32, (slots, bands), 1)
        spread = (slot // cap == owner).astype(F32)
        near = picks.shape[1]
        row = lax.broadcasted_iota(jnp.int32, (slots, cap * near), 0)
        lane = lax.broadcasted_iota(jnp.int32, (slots, cap * near), 1)
        own = lane // near == row % cap
        chosen = jnp.zeros((slots, REGION), F32)
        col = jnp.concatenate([picks[c] for c in range(cap)], axis=0).astype(F32)
        wt = jnp.concatenate([jnp.where(counts[...] > c, weights[c], 0.0) for c in range(cap)], axis=0)
        col = dot(spread, col, NT, HIGHEST)
        wt = dot(spread, wt, NT, HIGHEST)
        at = band_column(lax.broadcasted_iota(jnp.int32, (1, REGION), 1)).astype(F32)
        for k in range(near):
            here = own & (lane % near == k)
            col_k = jnp.sum(jnp.where(here, col, 0.0), axis=1, keepdims=True)
            wt_k = jnp.sum(jnp.where(here, wt, 0.0), axis=1, keepdims=True)
            chosen += jnp.where(jnp.abs(col_k - at) < 0.5, wt_k, 0.0)
        high, low = halves(chosen)
        select[0] = high
        select[1] = low

    def scale_jac(first, last):
        lane = lax.broadcasted_iota(jnp.int32, (cap, bands), 1)

        def body(q):
            jac_copy(q).wait()
            for n in range(channels):
                scale = jnp.sum(jnp.where(lane == q, errors[n], 0.0), axis=1, keepdims=True)
                jscaled[q, n] = jbuf[q, n] * scale

        loop(first, last, body)

    def back_table():
        g = hmat[:, :TILE]
        for _ in range(3):
            g = dot(hmat[...], g, precision=HIGHEST)
        high, low = halves(g)
        table[1, 0] = high
        table[1, 1] = low

    chain(0, (0, 1, 2, 3), src, [
        make_select, lambda: scale_jac(0, bands // 2), lambda: scale_jac(bands // 2, bands), back_table])

    def fold(x):
        count = x.shape[0] // cap
        x = x.reshape(count, cap, 384)
        last = x[:, :8, 256:] + pltpu.roll(x[:, 8:, 256:].reshape(count * 8, 128), 64, 1).reshape(count, 8, 128)
        return jnp.concatenate([x[:, :, :128], x[:, :, 128:256], last], axis=1)

    def unfold(x):
        count = x.shape[0]
        last = x[:, 2 * cap :]
        turned = pltpu.roll(last.reshape(count * 8, 128), 64, 1).reshape(count, 8, 128)
        last = jnp.concatenate([last, turned], axis=1)
        return jnp.concatenate([x[:, :cap], x[:, cap : 2 * cap], last], axis=2).reshape(count * cap, 384)

    collect(0, 0)
    collect(0, 1)
    high, low = halves(whole[0].reshape(FIELDS, REGION))
    spare = jnp.zeros((384 - FIELDS, REGION), BF16)
    state = (jnp.concatenate([high, spare], axis=0), jnp.concatenate([low, spare], axis=0))
    prof_out[...] = fold(dot3((select[0], select[1]), state, NT))

    def profile_copy(d):
        q = band_at(d)
        return remote(prof_out.at[q], prof_in.at[b], send_p.at[d], recv_p.at[d], (t, q))

    def profile_arrival(d):
        q = band_at(-d)
        return remote(prof_out.at[q], prof_in.at[q], send_p.at[d], recv_p.at[d], (t, q))

    def return_copy(d):
        q = band_at(-d)
        return remote(ret_out.at[q], ret_in.at[b], send_r.at[d], recv_r.at[d], (t, q))

    def return_arrival(d):
        q = band_at(d)
        return remote(ret_out.at[q], ret_in.at[q], send_r.at[d], recv_r.at[d], (t, q))

    loop(1, bands, lambda d: profile_copy(d).start())

    def work(q, packed):
        profile = unfold(packed[None])
        first = profile[:, :levels]
        second = pltpu.roll(profile[:, 128:], 256 - (SPAN - 128), 1)[:, :levels]
        sums = [jnp.zeros((cap, levels), F32)] * 2
        for n in range(channels):
            jn, jw = jbuf[q, n], jscaled[q, n]
            for v, p in enumerate((first, second)):
                hidden = jnp.sum(jn * p, axis=1, keepdims=True)
                sums[v] = sums[v] + jw * hidden
        spare = jnp.zeros((cap, 256 - levels), F32)
        one = jnp.concatenate([sums[0], spare], axis=1)
        two = pltpu.roll(jnp.concatenate([sums[1], spare], axis=1), SPAN - 128, 1)
        back = jnp.concatenate([one[:, :128], one[:, 128:] + two[:, :128], two[:, 128:]], axis=1)
        return fold(back)[0]

    ret_in[b] = work(b, prof_out[b])

    def serve(d):
        q = band_at(-d)
        profile_arrival(d).wait_recv()
        ret_out[q] = work(q, prof_in[q])
        return_copy(d).start()

    loop(1, bands, serve)
    loop(1, bands, lambda d: return_arrival(d).wait_recv())
    back = halves(jnp.swapaxes(unfold(ret_in[...]), 0, 1)[:FIELDS])
    seen = whole.at[2]
    seen[...] = dot3(back, (select[0], select[1])).reshape(2, SPAN, REGION)
    scatter(1, seen, 3)
    keep_own(1, seen)
    chain(1, (3, 2, 1, 0), seen, [None] * WINDOWS)
    for v in range(2):
        collect(1, v)
        x = thirds(whole[1, v])
        end = dot(x[0], order[...]) + (dot(x[1], order[...]) + dot(x[2], order[...]))
        for r in range(4):
            out[v, :, r, :] = end[:levels, r * 128 : (r + 1) * 128]

    for s, source in ((0, src), (1, seen)):
        for v in range(2):
            for d in (1, 2, 3):
                scatter_copy(s, source, d, v).wait_send()
            for k in range(WINDOWS):
                @pl.when(t != k)
                def _():
                    remote(ends.at[s, k, v], whole.at[s, v, :, mine], send_e.at[s, k, v],
                           recv_e.at[s, t, v], (k, b)).wait_send()
    for copy in started:
        copy.wait_send()

    def drain(d):
        return_copy(d).wait_send()
        profile_copy(d).wait_send()

    loop(1, bands, drain)


def run(bands, f, coupling, diff, picks, weights, counts, errors, jac):
    vmem = pl.BlockSpec(memory_space=pltpu.VMEM)
    dma = pltpu.SemaphoreType.DMA
    slots = bands * jac.shape[2]
    packed = pltpu.VMEM((bands, 40, 128), F32)
    return pl.pallas_call(
        functools.partial(whole_loop, bands),
        out_shape=jax.ShapeDtypeStruct(f.shape, F32),
        in_specs=[vmem] * 7 + [pl.BlockSpec(memory_space=pl.ANY)],
        out_specs=vmem,
        scratch_shapes=[
            pltpu.VMEM((REGION, REGION), BF16),
            pltpu.VMEM((2, SPAN, REGION), F32),
            pltpu.VMEM((2, WINDOWS, 2, SPAN, TILE), F32),
            pltpu.VMEM((2, WINDOWS, 2, SPAN, REGION), F32),
            pltpu.VMEM((2, WINDOWS, 2, 32, 256), F32),
            pltpu.VMEM((2, WINDOWS, 2, 128, 256), F32),
            pltpu.VMEM((2, WINDOWS, 2, SPAN, TILE), F32),
            pltpu.VMEM((3, 2, SPAN, REGION), F32),
            pltpu.VMEM((2, 4, 128), F32),
            pltpu.VMEM((REGION, REGION), F32),
            pltpu.VMEM((256, 256), F32),
            pltpu.VMEM((2, 2, SPAN, SPAN), BF16),
            pltpu.VMEM((2, 2, REGION, TILE), BF16),
            pltpu.VMEM(jac.shape, F32),
            pltpu.VMEM(jac.shape, F32),
            pltpu.VMEM((2, slots, REGION), BF16),
            packed, packed, packed, packed,
            dma((2, 2, 4)), dma((2, 4, 2)),
            dma((2, 4, 2, 8)), dma((2, 4, 2, 8)),
            dma((2, 4, 2)), dma((2, 4, 2)),
            dma((2,)), dma((2,)),
            dma((bands,)), dma((bands,)), dma((bands,)), dma((bands,)), dma((bands,)),
        ],
        compiler_params=pltpu.CompilerParams(
            collective_id=0, has_side_effects=True, vmem_limit_bytes=56 * 1024 * 1024,
        ),
        name="inner_loop",
    )(f, coupling, diff, picks, weights, counts, errors, jac)


def shards(forcing, coupling, diffusion, error_scale, pick_cols, pick_weights,
           send_count, jacobian, obs_weight):
    own = forcing[0]
    adjoint = run(
        lax.axis_size("lat"), own, coupling, diffusion,
        jnp.transpose(pick_cols[0, 0], (1, 2, 0)),
        jnp.transpose(pick_weights[0, 0], (1, 2, 0)),
        send_count[0],
        jnp.transpose(obs_weight[0, 0], (2, 1, 0)),
        jnp.transpose(jacobian[0, 0], (0, 2, 1, 3)),
    )
    return (adjoint + error_scale[None, :, None, None] * own)[None]


def solution(mesh):
    return jax.shard_map(
        shards,
        mesh=mesh,
        in_specs=(
            P("tm", None, None, "lat", None),
            P(),
            P("lat", None),
            P(),
            P("tm", "lat", None, None, None),
            P("tm", "lat", None, None, None),
            P("tm", "lat", None),
            P("tm", "lat", None, None, None, None),
            P("tm", "lat", None, None, None),
        ),
        out_specs=P("tm", None, None, "lat", None),
        check_vma=False,
    )
```

```python
import functools
import jax
import jax.numpy as jnp
from jax import lax
from jax.experimental import pallas as pl
from jax.experimental.pallas import tpu as pltpu
from jax.sharding import PartitionSpec as P

F32 = jnp.float32
BF16 = jnp.bfloat16
MESH = pl.DeviceIdType.MESH
HIGHEST = lax.Precision.HIGHEST
TILE = 128
REGION = 512
FIELDS = 288
SPAN = 144
WINDOWS = 4

NN = ((1,), (0,))
NT = ((1,), (1,))


def dot(a, b, dims=NN, precision=None):
    return lax.dot_general(
        a, b, (dims, ((), ())), precision=precision, preferred_element_type=F32
    )


def halves(x):
    high = x.astype(BF16)
    return high, (x - high.astype(F32)).astype(BF16)


def thirds(x):
    high = x.astype(BF16)
    rest = x - high.astype(F32)
    middle = rest.astype(BF16)
    return high, middle, (rest - middle.astype(F32)).astype(BF16)


def dot3(a, b, dims=NN):
    return dot(a[0], b[0], dims) + (dot(a[0], b[1], dims) + dot(a[1], b[0], dims))


def band_column(i):
    return ((i >> 2) & 3) * 128 + (i >> 7) * 32 + ((i >> 4) & 7) * 4 + (i & 3)


def region_place(i):
    block = i >> 7
    row = ((i >> 2) & 3) + jnp.where(block == 1, -4, jnp.where(block == 2, 4, 0))
    lon = ((i >> 4) & 7) * 4 + (i & 3)
    edge = (i - 384) >> 4
    edge_row = ((i >> 2) & 3) + jnp.where(edge < 2, 0, jnp.where(edge < 4, -4, 4))
    edge_lon = (i & 3) + jnp.where((edge & 1) == 0, -4, 32)
    return jnp.where(i < 384, row, edge_row), jnp.where(i < 384, lon, edge_lon)


def step_matrix(bands, band, part, above, here, below):
    i = lax.broadcasted_iota(jnp.int32, (REGION, 128), 0)
    lane = lax.broadcasted_iota(jnp.int32, (REGION, 128), 1)
    row_i, lon_i = region_place(i)
    rows = jnp.zeros((REGION, 128), F32)
    for source, first in ((above, -4), (here, 0), (below, 4)):
        for k in range(4):
            rows = jnp.where(row_i == first + k, source[k : k + 1, :], rows)
    picked = lane == ((lon_i + 32 * part) & 127)
    spread = jnp.sum(jnp.where(picked, rows, 0.0), axis=1, keepdims=True)
    i1 = lax.broadcasted_iota(jnp.int32, (REGION, 1), 0)
    j1 = lax.broadcasted_iota(jnp.int32, (1, REGION), 1)
    row_a, lon_a = region_place(i1)
    row_b, lon_b = region_place(j1)
    last = 4 * bands - 4 * band
    ok_a = (row_a >= -4 * band) & (row_a < last) & (i1 < 480)
    ok_b = (row_b >= -4 * band) & (row_b < last) & (j1 < 480)
    spread = jnp.where(ok_a, spread, 0.0)
    one = jnp.where(ok_a, 1.0, 0.0)
    apart = jnp.abs(row_a - row_b) + jnp.abs(lon_a - lon_b)
    h = jnp.where(apart == 0, one - 4.0 * spread, jnp.where(apart == 1, spread, 0.0))
    return jnp.where(ok_b, h, 0.0)


EDGES = ((2, 1, 1, 1), (3, 0, 1, -1), (4, 1, -1, 1), (5, 0, -1, -1), (0, 1, 0, 1), (1, 0, 0, -1))


def whole_loop(bands, f_hbm, coupling_hbm, diff_hbm, picks_hbm, weights_hbm, counts_hbm, errors_hbm, jac, out,
               f, coupling, diff, picks, weights, counts, errors, fetched, order, src, parts, region, own_edges, edges, ends, whole, dbuf, hmat, power,
               mixer, table, jbuf, jscaled, select, prof_out, prof_in, ret_out, ret_in,
               send_x, recv_x, send_h, recv_h, send_e, recv_e, send_d, recv_d,
               jsem, send_p, recv_p, send_r, recv_r):
    t, b = lax.axis_index("tm"), lax.axis_index("lat")
    channels, cap, levels = jac.shape[1:]
    mine = pl.ds(pl.multiple_of(t * TILE, TILE), TILE)

    def place(dt, db):
        return (lax.rem(t + dt + WINDOWS, WINDOWS), lax.rem(b + db + bands, bands))

    def band_at(d):
        return lax.rem(b + d + bands, bands)

    def remote(source, target, send, recv, device):
        return pltpu.make_async_remote_copy(
            src_ref=source, dst_ref=target, send_sem=send, recv_sem=recv,
            device_id=device, device_id_type=MESH,
        )

    def loop(first, last, body):
        def step(d, carry):
            body(d)
            return carry

        lax.fori_loop(first, last, step, 0)

    barrier = pltpu.get_barrier_semaphore()
    greeted = [(d, 0) for d in (1, 2, 3)] + [(d, s) for d in (-1, 1) for s in (-1, 1)]
    for dt, db in greeted:
        pl.semaphore_signal(barrier, inc=1, device_id=place(dt, db), device_id_type=MESH)
    loop(1, bands, lambda d: pl.semaphore_signal(
        barrier, inc=1, device_id=(t, band_at(d)), device_id_type=MESH))

    fetches = []
    for k, (source, target) in enumerate((
            (f_hbm, f), (coupling_hbm, coupling), (diff_hbm, diff), (picks_hbm, picks),
            (weights_hbm, weights), (counts_hbm, counts), (errors_hbm, errors))):
        fetches.append(pltpu.make_async_copy(source, target, fetched.at[k]))
        fetches[-1].start()

    def jac_copy(q):
        return pltpu.make_async_copy(jac.at[q], jbuf.at[q], jsem.at[q])

    loop(0, bands, lambda q: jac_copy(q).start())

    place_i = band_column(lax.broadcasted_iota(jnp.int32, (REGION, 1), 0))
    column = lax.broadcasted_iota(jnp.int32, (1, REGION), 1)
    order[...] = (place_i == column).astype(F32).astype(BF16)
    for copy in fetches:
        copy.wait()
    for v in range(2):
        src[v, 136:, :] = jnp.zeros((8, REGION), F32)
        for r in range(4):
            src[v, :levels, r * 128 : (r + 1) * 128] = f[v, :, r, :]
        x = thirds(src[v])
        src[v] = dot(x[0], order[...], NT) + (dot(x[1], order[...], NT) + dot(x[2], order[...], NT))

    pl.semaphore_wait(barrier, len(greeted) + bands - 1)

    spreads = [remote(diff, dbuf.at[k], send_d.at[k], recv_d.at[k], place(0, s))
               for k, s in ((0, 1), (1, -1))]
    for copy in spreads:
        copy.start()

    started = []

    def scatter_copy(s, source, d, v):
        to = lax.rem(t + d, WINDOWS)
        return remote(source.at[v, :, pl.ds(pl.multiple_of(to * TILE, TILE), TILE)],
                      parts.at[s, t, v], send_x.at[s, v, d], recv_x.at[s, t, v], (to, b))

    def scatter(s, source):
        for v in range(2):
            for d in (2, 1, 3):
                scatter_copy(s, source, d, v).start()
        for v in range(2):
            parts[s, t, v] = source[v, :, mine]

    scatter(0, src)

    for s in range(2):
        for w in range(WINDOWS):
            for v in range(2):
                edges[s, w, v, 96:, :] = jnp.zeros((32, 256), F32)
    eye = (lax.broadcasted_iota(jnp.int32, (levels, levels), 0)
           == lax.broadcasted_iota(jnp.int32, (levels, levels), 1)).astype(F32)
    mix = 0.8 * eye + 0.2 * coupling[...]
    twice = dot(mix, mix, precision=HIGHEST)
    power[...] = jnp.zeros((256, 256), F32)
    power[:levels, :levels] = dot(twice, twice, precision=HIGHEST)
    for s in range(2):
        full = power[...] if s == 0 else jnp.swapaxes(power[...], 0, 1)
        high, low = halves(full[:SPAN, :SPAN])
        mixer[s, 0] = high
        mixer[s, 1] = low

    for copy in spreads:
        copy.wait()
    hmat[...] = step_matrix(bands, b, t, dbuf[0], diff[...], dbuf[1])
    g = hmat[:TILE, :]
    for _ in range(3):
        g = dot(g, hmat[...], precision=HIGHEST)
    high, low = halves(jnp.swapaxes(g, 0, 1))
    table[0, 0] = high
    table[0, 1] = low

    edge_i = lax.broadcasted_iota(jnp.int32, (32, TILE), 0)
    edge_j = lax.broadcasted_iota(jnp.int32, (32, TILE), 1)
    edge_of = (edge_j == jnp.where(edge_i < 16, edge_i, edge_i + 96)).astype(F32).astype(BF16)

    def halo_copies(s, w, v):
        copies = []
        for at, side, db, dt in EDGES:
            copies.append(remote(own_edges.at[s, w, v, pl.ds(16 * side, 16)],
                                 edges.at[s, w, v, pl.ds(16 * at, 16)],
                                 send_h.at[s, w, v, at], recv_h.at[s, w, v, at], place(dt, db)))
        for k, db in ((1, 1), (2, -1)):
            copies.append(remote(region.at[s, w, v, :, pl.ds(0, TILE)],
                                 region.at[s, w, v, :, pl.ds(k * TILE, TILE)],
                                 send_h.at[s, w, v, 5 + k], recv_h.at[s, w, v, 5 + k], place(0, db)))
        return copies

    def send_halo(s, w, before, v):
        @pl.when(t != w)
        def _():
            remote(parts.at[s, w, v], parts.at[s, w, v], send_x.at[s, v, 0], recv_x.at[s, w, v],
                   (t, b)).wait_recv()

        state = parts[s, w, v]
        if before is not None:
            state = state + ends[s, before, v]
        mixed = dot3((mixer[s, 0], mixer[s, 1]), halves(state))
        center = halves(mixed)
        own_edges[s, w, v, :, :SPAN] = dot(edge_of, center[0], NT) + dot(edge_of, center[1], NT)
        region[s, w, v, :, :TILE] = mixed
        copies = halo_copies(s, w, v)
        for copy in copies:
            copy.start()
        started.extend(copies)
        ends[s, w, v] = dot3(center, (table[s, 0, :TILE], table[s, 1, :TILE]))

    def receive_halo(s, w, v):
        for copy in halo_copies(s, w, v):
            copy.wait_recv()
        region[s, w, v, :, 384:] = jnp.swapaxes(edges[s, w, v], 0, 1)[:SPAN]
        ends[s, w, v] += dot3(halves(region[s, w, v, :, TILE:]),
                              (table[s, 0, TILE:], table[s, 1, TILE:]))

    def send_end(s, w, v):
        @pl.when(t != w)
        def _():
            remote(ends.at[s, w, v], whole.at[s, v, :, mine], send_e.at[s, w, v],
                   recv_e.at[s, t, v], (w, b)).start()

        @pl.when(t == w)
        def _():
            whole[s, v, :, mine] = ends[s, w, v]

    def chain(s, windows, beside):
        for v in range(2):
            send_halo(s, windows[0], None, v)
        for k, w in enumerate(windows):
            if beside[k] is not None:
                beside[k]()
            for v in range(2):
                receive_halo(s, w, v)
                if k < WINDOWS - 1:
                    send_halo(s, windows[k + 1], w, v)
                else:
                    send_end(s, w, v)
        for w in windows[-2::-1]:
            for v in range(2):
                send_end(s, w, v)

    def collect(s, v):
        for k in range(WINDOWS):
            @pl.when(t != k)
            def _():
                piece = whole.at[s, v, :, pl.ds(k * TILE, TILE)]
                remote(piece, piece, send_e.at[s, k, v], recv_e.at[s, k, v], (t, b)).wait_recv()

    slots = bands * cap

    def make_select():
        slot = lax.broadcasted_iota(jnp.int32, (slots, bands), 0)
        owner = lax.broadcasted_iota(jnp.int32, (slots, bands), 1)
        spread = (slot // cap == owner).astype(F32)
        near = picks.shape[1]
        row = lax.broadcasted_iota(jnp.int32, (slots, cap * near), 0)
        lane = lax.broadcasted_iota(jnp.int32, (slots, cap * near), 1)
        own = lane // near == row % cap
        chosen = jnp.zeros((slots, REGION), F32)
        col = jnp.concatenate([picks[c] for c in range(cap)], axis=0).astype(F32)
        wt = jnp.concatenate([jnp.where(counts[...] > c, weights[c], 0.0) for c in range(cap)], axis=0)
        col = dot(spread, col, NT, HIGHEST)
        wt = dot(spread, wt, NT, HIGHEST)
        at = band_column(lax.broadcasted_iota(jnp.int32, (1, REGION), 1)).astype(F32)
        for k in range(near):
            here = own & (lane % near == k)
            col_k = jnp.sum(jnp.where(here, col, 0.0), axis=1, keepdims=True)
            wt_k = jnp.sum(jnp.where(here, wt, 0.0), axis=1, keepdims=True)
            chosen += jnp.where(jnp.abs(col_k - at) < 0.5, wt_k, 0.0)
        high, low = halves(chosen)
        select[0] = high
        select[1] = low

    def scale_jac(first, last):
        lane = lax.broadcasted_iota(jnp.int32, (cap, bands), 1)

        def body(q):
            jac_copy(q).wait()
            for n in range(channels):
                scale = jnp.sum(jnp.where(lane == q, errors[n], 0.0), axis=1, keepdims=True)
                jscaled[q, n] = jbuf[q, n] * scale

        loop(first, last, body)

    def back_table():
        g = hmat[:, :TILE]
        for _ in range(3):
            g = dot(hmat[...], g, precision=HIGHEST)
        high, low = halves(g)
        table[1, 0] = high
        table[1, 1] = low

    chain(0, (0, 1, 2, 3), [
        make_select, lambda: scale_jac(0, bands // 2), lambda: scale_jac(bands // 2, bands), back_table])

    def fold(x):
        count = x.shape[0] // cap
        x = x.reshape(count, cap, 384)
        last = x[:, :8, 256:] + pltpu.roll(x[:, 8:, 256:].reshape(count * 8, 128), 64, 1).reshape(count, 8, 128)
        return jnp.concatenate([x[:, :, :128], x[:, :, 128:256], last], axis=1)

    def unfold(x):
        count = x.shape[0]
        last = x[:, 2 * cap :]
        turned = pltpu.roll(last.reshape(count * 8, 128), 64, 1).reshape(count, 8, 128)
        last = jnp.concatenate([last, turned], axis=1)
        return jnp.concatenate([x[:, :cap], x[:, cap : 2 * cap], last], axis=2).reshape(count * cap, 384)

    collect(0, 0)
    collect(0, 1)
    high, low = halves(whole[0].reshape(FIELDS, REGION))
    spare = jnp.zeros((384 - FIELDS, REGION), BF16)
    state = (jnp.concatenate([high, spare], axis=0), jnp.concatenate([low, spare], axis=0))
    prof_out[...] = fold(dot3((select[0], select[1]), state, NT))

    across = min(4, bands // 2)
    down = bands // (2 * across)

    def far_first(j, size):
        if size == 4:
            return lax.rem(2 + 3 * j + 3 * (j * (j - 1) // 2), 4)
        return size - 1 - j

    def partner(d, sign):
        core = lax.rem(b + d + 1, 2)
        dy = far_first(lax.rem(d // 2, across), across)
        dx = far_first(d // (2 * across), down)
        y = lax.rem(lax.rem(b // 2, across) + sign * dy + across, across)
        x = lax.rem(b // (2 * across) + sign * dx + down, down)
        return (x * across + y) * 2 + core

    def profile_copy(d):
        q = partner(d, 1)
        return remote(prof_out.at[q], prof_in.at[b], send_p.at[d], recv_p.at[d], (t, q))

    def profile_arrival(d):
        q = partner(d, -1)
        return remote(prof_out.at[q], prof_in.at[q], send_p.at[d], recv_p.at[d], (t, q))

    def return_copy(d):
        q = partner(d, -1)
        return remote(ret_out.at[q], ret_in.at[b], send_r.at[d], recv_r.at[d], (t, q))

    def return_arrival(d):
        q = partner(d, 1)
        return remote(ret_out.at[q], ret_in.at[q], send_r.at[d], recv_r.at[d], (t, q))

    loop(0, bands - 1, lambda d: profile_copy(d).start())

    def work(q, packed):
        profile = unfold(packed[None])
        first = profile[:, :levels]
        second = pltpu.roll(profile[:, 128:], 256 - (SPAN - 128), 1)[:, :levels]
        sums = [jnp.zeros((cap, levels), F32)] * 2
        for n in range(channels):
            jn, jw = jbuf[q, n], jscaled[q, n]
            for v, p in enumerate((first, second)):
                hidden = jnp.sum(jn * p, axis=1, keepdims=True)
                sums[v] = sums[v] + jw * hidden
        spare = jnp.zeros((cap, 256 - levels), F32)
        one = jnp.concatenate([sums[0], spare], axis=1)
        two = pltpu.roll(jnp.concatenate([sums[1], spare], axis=1), SPAN - 128, 1)
        back = jnp.concatenate([one[:, :128], one[:, 128:] + two[:, :128], two[:, 128:]], axis=1)
        return fold(back)[0]

    ret_in[b] = work(b, prof_out[b])

    def serve(d):
        q = partner(d, -1)
        profile_arrival(d).wait_recv()
        ret_out[q] = work(q, prof_in[q])
        return_copy(d).start()

    loop(0, bands - 1, serve)
    loop(0, bands - 1, lambda d: return_arrival(d).wait_recv())
    back = halves(jnp.swapaxes(unfold(ret_in[...]), 0, 1)[:FIELDS])
    seen = whole.at[2]
    seen[...] = dot3(back, (select[0], select[1])).reshape(2, SPAN, REGION)
    scatter(1, seen)
    chain(1, (3, 2, 1, 0), [None] * WINDOWS)
    for v in range(2):
        collect(1, v)
        x = thirds(whole[1, v])
        end = dot(x[0], order[...]) + (dot(x[1], order[...]) + dot(x[2], order[...]))
        for r in range(4):
            out[v, :, r, :] = end[:levels, r * 128 : (r + 1) * 128]

    for s, source in ((0, src), (1, seen)):
        for v in range(2):
            for d in (1, 2, 3):
                scatter_copy(s, source, d, v).wait_send()
            for k in range(WINDOWS):
                @pl.when(t != k)
                def _():
                    remote(ends.at[s, k, v], whole.at[s, v, :, mine], send_e.at[s, k, v],
                           recv_e.at[s, t, v], (k, b)).wait_send()
    for copy in started:
        copy.wait_send()

    def drain(d):
        return_copy(d).wait_send()
        profile_copy(d).wait_send()

    loop(0, bands - 1, drain)


def run(bands, f, coupling, diff, picks, weights, counts, errors, jac):
    vmem = pl.BlockSpec(memory_space=pltpu.VMEM)
    dma = pltpu.SemaphoreType.DMA
    slots = bands * jac.shape[2]
    packed = pltpu.VMEM((bands, 40, 128), F32)
    return pl.pallas_call(
        functools.partial(whole_loop, bands),
        out_shape=jax.ShapeDtypeStruct(f.shape, F32),
        in_specs=[pl.BlockSpec(memory_space=pl.ANY)] * 8,
        out_specs=vmem,
        scratch_shapes=[
            pltpu.VMEM(x.shape, x.dtype)
            for x in (f, coupling, diff, picks, weights, counts, errors)
        ] + [
            dma((7,)),
            pltpu.VMEM((REGION, REGION), BF16),
            pltpu.VMEM((2, SPAN, REGION), F32),
            pltpu.VMEM((2, WINDOWS, 2, SPAN, TILE), F32),
            pltpu.VMEM((2, WINDOWS, 2, SPAN, REGION), F32),
            pltpu.VMEM((2, WINDOWS, 2, 32, 256), F32),
            pltpu.VMEM((2, WINDOWS, 2, 128, 256), F32),
            pltpu.VMEM((2, WINDOWS, 2, SPAN, TILE), F32),
            pltpu.VMEM((3, 2, SPAN, REGION), F32),
            pltpu.VMEM((2, 4, 128), F32),
            pltpu.VMEM((REGION, REGION), F32),
            pltpu.VMEM((256, 256), F32),
            pltpu.VMEM((2, 2, SPAN, SPAN), BF16),
            pltpu.VMEM((2, 2, REGION, TILE), BF16),
            pltpu.VMEM(jac.shape, F32),
            pltpu.VMEM(jac.shape, F32),
            pltpu.VMEM((2, slots, REGION), BF16),
            packed, packed, packed, packed,
            dma((2, 2, 4)), dma((2, 4, 2)),
            dma((2, 4, 2, 8)), dma((2, 4, 2, 8)),
            dma((2, 4, 2)), dma((2, 4, 2)),
            dma((2,)), dma((2,)),
            dma((bands,)), dma((bands,)), dma((bands,)), dma((bands,)), dma((bands,)),
        ],
        compiler_params=pltpu.CompilerParams(
            collective_id=0, has_side_effects=True, vmem_limit_bytes=56 * 1024 * 1024,
        ),
        name="inner_loop",
    )(f, coupling, diff, picks, weights, counts, errors, jac)


def shards(forcing, coupling, diffusion, error_scale, pick_cols, pick_weights,
           send_count, jacobian, obs_weight):
    own = forcing[0]
    adjoint = run(
        lax.axis_size("lat"), own, coupling, diffusion,
        jnp.transpose(pick_cols[0, 0], (1, 2, 0)),
        jnp.transpose(pick_weights[0, 0], (1, 2, 0)),
        send_count[0],
        jnp.transpose(obs_weight[0, 0], (2, 1, 0)),
        jnp.transpose(jacobian[0, 0], (0, 2, 1, 3)),
    )
    return (adjoint + error_scale[None, :, None, None] * own)[None]


def solution(mesh):
    return jax.shard_map(
        shards,
        mesh=mesh,
        in_specs=(
            P("tm", None, None, "lat", None),
            P(),
            P("lat", None),
            P(),
            P("tm", "lat", None, None, None),
            P("tm", "lat", None, None, None),
            P("tm", "lat", None),
            P("tm", "lat", None, None, None, None),
            P("tm", "lat", None, None, None),
        ),
        out_specs=P("tm", None, None, "lat", None),
        check_vma=False,
    )
```

```python
import functools
import jax
import jax.numpy as jnp
from jax import lax
from jax.experimental import pallas as pl
from jax.experimental.pallas import tpu as pltpu
from jax.sharding import PartitionSpec as P

F32 = jnp.float32
BF16 = jnp.bfloat16
MESH = pl.DeviceIdType.MESH
HIGHEST = lax.Precision.HIGHEST
TILE = 128
REGION = 512
FIELDS = 288
SPAN = 144
WINDOWS = 4

NN = ((1,), (0,))
NT = ((1,), (1,))


def dot(a, b, dims=NN, precision=None):
    return lax.dot_general(
        a, b, (dims, ((), ())), precision=precision, preferred_element_type=F32
    )


def halves(x):
    high = x.astype(BF16)
    return high, (x - high.astype(F32)).astype(BF16)


def thirds(x):
    high = x.astype(BF16)
    rest = x - high.astype(F32)
    middle = rest.astype(BF16)
    return high, middle, (rest - middle.astype(F32)).astype(BF16)


def dot3(a, b, dims=NN):
    return dot(a[0], b[0], dims) + (dot(a[0], b[1], dims) + dot(a[1], b[0], dims))


def band_column(i):
    return ((i >> 2) & 3) * 128 + (i >> 7) * 32 + ((i >> 4) & 7) * 4 + (i & 3)


def corner_cell(j):
    down = jnp.where(j < 3, 1, jnp.where(j < 5, 2, 3))
    return down, jnp.where(j < 3, j + 1, jnp.where(j < 5, j - 2, j - 4))


def region_place(i):
    block = i >> 7
    row = ((i >> 2) & 3) + jnp.where(block == 1, -4, jnp.where(block == 2, 4, 0))
    lon = ((i >> 4) & 7) * 4 + (i & 3)
    k = i - 384
    side_lon = (i & 3) + jnp.where(k < 16, -4, 32)
    corner = (k - 32) >> 3
    dr, dl = corner_cell(k & 7)
    corner_row = jnp.where(corner < 2, -dr, 3 + dr)
    corner_lon = jnp.where((corner & 1) == 0, -dl, 31 + dl)
    row = jnp.where(i < 416, jnp.where(i < 384, row, (i >> 2) & 3), corner_row)
    return row, jnp.where(i < 384, lon, jnp.where(i < 416, side_lon, corner_lon))


def region_used(i):
    return (i < 416) | ((i < 448) & ((i & 7) < 6))


def edge_column(i):
    side = jnp.where(i < 16, i, i + 96)
    corner = (i - 32) >> 3
    dr, dl = corner_cell(i & 7)
    row = jnp.where(corner < 2, 4 - dr, dr - 1)
    lon = jnp.where((corner & 1) == 0, 32 - dl, dl - 1)
    return jnp.where(i < 32, side, (lon >> 2) * 16 + row * 4 + (lon & 3))


def step_matrix(bands, band, part, above, here, below):
    i = lax.broadcasted_iota(jnp.int32, (REGION, 128), 0)
    lane = lax.broadcasted_iota(jnp.int32, (REGION, 128), 1)
    row_i, lon_i = region_place(i)
    rows = jnp.zeros((REGION, 128), F32)
    for source, first in ((above, -4), (here, 0), (below, 4)):
        for k in range(4):
            rows = jnp.where(row_i == first + k, source[k : k + 1, :], rows)
    picked = lane == ((lon_i + 32 * part) & 127)
    spread = jnp.sum(jnp.where(picked, rows, 0.0), axis=1, keepdims=True)
    i1 = lax.broadcasted_iota(jnp.int32, (REGION, 1), 0)
    j1 = lax.broadcasted_iota(jnp.int32, (1, REGION), 1)
    row_a, lon_a = region_place(i1)
    row_b, lon_b = region_place(j1)
    last = 4 * bands - 4 * band
    ok_a = (row_a >= -4 * band) & (row_a < last) & region_used(i1)
    ok_b = (row_b >= -4 * band) & (row_b < last) & region_used(j1)
    spread = jnp.where(ok_a, spread, 0.0)
    one = jnp.where(ok_a, 1.0, 0.0)
    apart = jnp.abs(row_a - row_b) + jnp.abs(lon_a - lon_b)
    h = jnp.where(apart == 0, one - 4.0 * spread, jnp.where(apart == 1, spread, 0.0))
    return jnp.where(ok_b, h, 0.0)


EDGES = (
    (32, 32, 8, 1, 1),
    (40, 40, 8, 1, -1),
    (48, 48, 8, -1, 1),
    (56, 56, 8, -1, -1),
    (0, 16, 16, 0, 1),
    (16, 0, 16, 0, -1),
)


def whole_loop(bands, f_hbm, coupling_hbm, diff_hbm, picks_hbm, weights_hbm, counts_hbm, errors_hbm, jac, out,
               f, coupling, diff, picks, weights, counts, errors, fetched, order, src, parts, region, own_edges, edges, ends, whole, dbuf, hmat, power,
               mixer, table, jbuf, jscaled, select, prof_out, prof_in, ret_out, ret_in,
               send_x, recv_x, send_h, recv_h, send_e, recv_e, send_d, recv_d,
               jsem, send_p, recv_p, send_r, recv_r):
    t, b = lax.axis_index("tm"), lax.axis_index("lat")
    channels, cap, levels = jac.shape[1:]
    mine = pl.ds(pl.multiple_of(t * TILE, TILE), TILE)

    def place(dt, db):
        return (lax.rem(t + dt + WINDOWS, WINDOWS), lax.rem(b + db + bands, bands))

    def band_at(d):
        return lax.rem(b + d + bands, bands)

    def remote(source, target, send, recv, device):
        return pltpu.make_async_remote_copy(
            src_ref=source, dst_ref=target, send_sem=send, recv_sem=recv,
            device_id=device, device_id_type=MESH,
        )

    def loop(first, last, body):
        def step(d, carry):
            body(d)
            return carry

        lax.fori_loop(first, last, step, 0)

    barrier = pltpu.get_barrier_semaphore()
    greeted = [(d, 0) for d in (1, 2, 3)] + [(d, s) for d in (-1, 1) for s in (-1, 1)]
    for dt, db in greeted:
        pl.semaphore_signal(barrier, inc=1, device_id=place(dt, db), device_id_type=MESH)
    loop(1, bands, lambda d: pl.semaphore_signal(
        barrier, inc=1, device_id=(t, band_at(d)), device_id_type=MESH))

    fetches = []
    for k, (source, target) in enumerate((
            (f_hbm, f), (coupling_hbm, coupling), (diff_hbm, diff), (picks_hbm, picks),
            (weights_hbm, weights), (counts_hbm, counts), (errors_hbm, errors))):
        fetches.append(pltpu.make_async_copy(source, target, fetched.at[k]))
        fetches[-1].start()

    def jac_copy(q):
        return pltpu.make_async_copy(jac.at[q], jbuf.at[q], jsem.at[q])

    loop(0, bands, lambda q: jac_copy(q).start())

    place_i = band_column(lax.broadcasted_iota(jnp.int32, (REGION, 1), 0))
    column = lax.broadcasted_iota(jnp.int32, (1, REGION), 1)
    order[...] = (place_i == column).astype(F32).astype(BF16)
    for copy in fetches:
        copy.wait()
    for v in range(2):
        src[v, 136:, :] = jnp.zeros((8, REGION), F32)
        for r in range(4):
            src[v, :levels, r * 128 : (r + 1) * 128] = f[v, :, r, :]
        x = thirds(src[v])
        src[v] = dot(x[0], order[...], NT) + (dot(x[1], order[...], NT) + dot(x[2], order[...], NT))

    pl.semaphore_wait(barrier, len(greeted) + bands - 1)

    spreads = [remote(diff, dbuf.at[k], send_d.at[k], recv_d.at[k], place(0, s))
               for k, s in ((0, 1), (1, -1))]
    for copy in spreads:
        copy.start()

    started = []

    def scatter_copy(s, source, d, v):
        to = lax.rem(t + d, WINDOWS)
        return remote(source.at[v, :, pl.ds(pl.multiple_of(to * TILE, TILE), TILE)],
                      parts.at[s, t, v], send_x.at[s, v, d], recv_x.at[s, t, v], (to, b))

    def scatter(s, source):
        for v in range(2):
            for d in (2, 1, 3):
                scatter_copy(s, source, d, v).start()
        for v in range(2):
            parts[s, t, v] = source[v, :, mine]

    scatter(0, src)

    for s in range(2):
        for w in range(WINDOWS):
            for v in range(2):
                edges[s, w, v, 64:, :] = jnp.zeros((64, 256), F32)
    eye = (lax.broadcasted_iota(jnp.int32, (levels, levels), 0)
           == lax.broadcasted_iota(jnp.int32, (levels, levels), 1)).astype(F32)
    mix = 0.8 * eye + 0.2 * coupling[...]
    twice = dot(mix, mix, precision=HIGHEST)
    power[...] = jnp.zeros((256, 256), F32)
    power[:levels, :levels] = dot(twice, twice, precision=HIGHEST)
    for s in range(2):
        full = power[...] if s == 0 else jnp.swapaxes(power[...], 0, 1)
        high, low = halves(full[:SPAN, :SPAN])
        mixer[s, 0] = high
        mixer[s, 1] = low

    def ahead_table():
        for copy in spreads:
            copy.wait()
        hmat[...] = step_matrix(bands, b, t, dbuf[0], diff[...], dbuf[1])
        g = hmat[:TILE, :]
        for _ in range(3):
            g = dot(g, hmat[...], precision=HIGHEST)
        high, low = halves(jnp.swapaxes(g, 0, 1))
        table[0, 0] = high
        table[0, 1] = low

    edge_i = edge_column(lax.broadcasted_iota(jnp.int32, (64, TILE), 0))
    edge_j = lax.broadcasted_iota(jnp.int32, (64, TILE), 1)
    edge_of = (edge_j == edge_i).astype(F32).astype(BF16)

    def halo_copies(s, w, v):
        copies = []
        for k, (at, start, size, db, dt) in enumerate(EDGES):
            copies.append(remote(own_edges.at[s, w, v, pl.ds(start, size)],
                                 edges.at[s, w, v, pl.ds(at, size)],
                                 send_h.at[s, w, v, k], recv_h.at[s, w, v, k], place(dt, db)))
        for k, db in ((1, 1), (2, -1)):
            copies.append(remote(region.at[s, w, v, :, pl.ds(0, TILE)],
                                 region.at[s, w, v, :, pl.ds(k * TILE, TILE)],
                                 send_h.at[s, w, v, 5 + k], recv_h.at[s, w, v, 5 + k], place(0, db)))
        return copies

    def send_halo(s, w, before, v):
        @pl.when(t != w)
        def _():
            remote(parts.at[s, w, v], parts.at[s, w, v], send_x.at[s, v, 0], recv_x.at[s, w, v],
                   (t, b)).wait_recv()

        state = parts[s, w, v]
        if before is not None:
            state = state + ends[s, before, v]
        mixed = dot3((mixer[s, 0], mixer[s, 1]), halves(state))
        center = halves(mixed)
        own_edges[s, w, v, :, :SPAN] = dot(edge_of, center[0], NT) + dot(edge_of, center[1], NT)
        region[s, w, v, :, :TILE] = mixed
        copies = halo_copies(s, w, v)
        for copy in copies:
            copy.start()
        started.extend(copies)

    def receive_halo(s, w, v):
        for copy in halo_copies(s, w, v):
            copy.wait_recv()
        region[s, w, v, :, 384:] = jnp.swapaxes(edges[s, w, v], 0, 1)[:SPAN]
        ends[s, w, v] = dot3(halves(region[s, w, v]), (table[s, 0], table[s, 1]))

    def send_end(s, w, v):
        @pl.when(t != w)
        def _():
            remote(ends.at[s, w, v], whole.at[s, v, :, mine], send_e.at[s, w, v],
                   recv_e.at[s, t, v], (w, b)).start()

        @pl.when(t == w)
        def _():
            whole[s, v, :, mine] = ends[s, w, v]

    def chain(s, windows, beside):
        for v in range(2):
            send_halo(s, windows[0], None, v)
        for k, w in enumerate(windows):
            if beside[k] is not None:
                beside[k]()
            for v in range(2):
                receive_halo(s, w, v)
                if k < WINDOWS - 1:
                    send_halo(s, windows[k + 1], w, v)
                else:
                    send_end(s, w, v)
        for w in windows[-2::-1]:
            for v in range(2):
                send_end(s, w, v)

    def collect(s, v):
        for k in range(WINDOWS):
            @pl.when(t != k)
            def _():
                piece = whole.at[s, v, :, pl.ds(k * TILE, TILE)]
                remote(piece, piece, send_e.at[s, k, v], recv_e.at[s, k, v], (t, b)).wait_recv()

    slots = bands * cap

    def make_select():
        slot = lax.broadcasted_iota(jnp.int32, (slots, bands), 0)
        owner = lax.broadcasted_iota(jnp.int32, (slots, bands), 1)
        spread = (slot // cap == owner).astype(F32)
        near = picks.shape[1]
        row = lax.broadcasted_iota(jnp.int32, (slots, cap * near), 0)
        lane = lax.broadcasted_iota(jnp.int32, (slots, cap * near), 1)
        own = lane // near == row % cap
        chosen = jnp.zeros((slots, REGION), F32)
        col = jnp.concatenate([picks[c] for c in range(cap)], axis=0).astype(F32)
        wt = jnp.concatenate([jnp.where(counts[...] > c, weights[c], 0.0) for c in range(cap)], axis=0)
        col = dot(spread, col, NT, HIGHEST)
        wt = dot(spread, wt, NT, HIGHEST)
        at = band_column(lax.broadcasted_iota(jnp.int32, (1, REGION), 1)).astype(F32)
        for k in range(near):
            here = own & (lane % near == k)
            col_k = jnp.sum(jnp.where(here, col, 0.0), axis=1, keepdims=True)
            wt_k = jnp.sum(jnp.where(here, wt, 0.0), axis=1, keepdims=True)
            chosen += jnp.where(jnp.abs(col_k - at) < 0.5, wt_k, 0.0)
        high, low = halves(chosen)
        select[0] = high
        select[1] = low

    def scale_jac(first, last):
        lane = lax.broadcasted_iota(jnp.int32, (cap, bands), 1)

        def body(q):
            jac_copy(q).wait()
            for n in range(channels):
                scale = jnp.sum(jnp.where(lane == q, errors[n], 0.0), axis=1, keepdims=True)
                jscaled[q, n] = jbuf[q, n] * scale

        loop(first, last, body)

    def back_table():
        g = hmat[:, :TILE]
        for _ in range(3):
            g = dot(hmat[...], g, precision=HIGHEST)
        high, low = halves(g)
        table[1, 0] = high
        table[1, 1] = low

    chain(0, (0, 1, 2, 3), [
        ahead_table, make_select, lambda: scale_jac(0, bands), back_table])

    def fold(x):
        count = x.shape[0] // cap
        x = x.reshape(count, cap, 384)
        last = x[:, :8, 256:] + pltpu.roll(x[:, 8:, 256:].reshape(count * 8, 128), 64, 1).reshape(count, 8, 128)
        return jnp.concatenate([x[:, :, :128], x[:, :, 128:256], last], axis=1)

    def unfold(x):
        count = x.shape[0]
        last = x[:, 2 * cap :]
        turned = pltpu.roll(last.reshape(count * 8, 128), 64, 1).reshape(count, 8, 128)
        last = jnp.concatenate([last, turned], axis=1)
        return jnp.concatenate([x[:, :cap], x[:, cap : 2 * cap], last], axis=2).reshape(count * cap, 384)

    collect(0, 0)
    collect(0, 1)
    high, low = halves(whole[0].reshape(FIELDS, REGION))
    spare = jnp.zeros((384 - FIELDS, REGION), BF16)
    state = (jnp.concatenate([high, spare], axis=0), jnp.concatenate([low, spare], axis=0))
    prof_out[...] = fold(dot3((select[0], select[1]), state, NT))

    across = min(4, bands // 2)
    down = bands // (2 * across)

    def far_first(j, size):
        if size == 4:
            return lax.rem(2 + 3 * j + 3 * (j * (j - 1) // 2), 4)
        return size - 1 - j

    def partner(d, sign):
        core = lax.rem(b + d + 1, 2)
        dy = far_first(lax.rem(d // 2, across), across)
        dx = far_first(d // (2 * across), down)
        y = lax.rem(lax.rem(b // 2, across) + sign * dy + across, across)
        x = lax.rem(b // (2 * across) + sign * dx + down, down)
        return (x * across + y) * 2 + core

    def profile_copy(d):
        q = partner(d, 1)
        return remote(prof_out.at[q], prof_in.at[b], send_p.at[d], recv_p.at[d], (t, q))

    def profile_arrival(d):
        q = partner(d, -1)
        return remote(prof_out.at[q], prof_in.at[q], send_p.at[d], recv_p.at[d], (t, q))

    def return_copy(d):
        q = partner(d, -1)
        return remote(ret_out.at[q], ret_in.at[b], send_r.at[d], recv_r.at[d], (t, q))

    def return_arrival(d):
        q = partner(d, 1)
        return remote(ret_out.at[q], ret_in.at[q], send_r.at[d], recv_r.at[d], (t, q))

    profile_copy(bands - 2).start()
    loop(0, bands - 2, lambda d: profile_copy(d).start())

    def work(q, packed):
        profile = unfold(packed[None])
        first = profile[:, :levels]
        second = pltpu.roll(profile[:, 128:], 256 - (SPAN - 128), 1)[:, :levels]
        sums = [jnp.zeros((cap, levels), F32)] * 2
        for n in range(channels):
            jn, jw = jbuf[q, n], jscaled[q, n]
            for v, p in enumerate((first, second)):
                hidden = jnp.sum(jn * p, axis=1, keepdims=True)
                sums[v] = sums[v] + jw * hidden
        spare = jnp.zeros((cap, 256 - levels), F32)
        one = jnp.concatenate([sums[0], spare], axis=1)
        two = pltpu.roll(jnp.concatenate([sums[1], spare], axis=1), SPAN - 128, 1)
        back = jnp.concatenate([one[:, :128], one[:, 128:] + two[:, :128], two[:, 128:]], axis=1)
        return fold(back)[0]

    ret_in[b] = work(b, prof_out[b])

    def serve(d):
        q = partner(d, -1)
        profile_arrival(d).wait_recv()
        ret_out[q] = work(q, prof_in[q])
        return_copy(d).start()

    serve(bands - 2)
    loop(0, bands - 2, serve)
    loop(0, bands - 1, lambda d: return_arrival(d).wait_recv())
    back = halves(jnp.swapaxes(unfold(ret_in[...]), 0, 1)[:FIELDS])
    seen = whole.at[2]
    seen[...] = dot3(back, (select[0], select[1])).reshape(2, SPAN, REGION)
    scatter(1, seen)
    chain(1, (3, 2, 1, 0), [None] * WINDOWS)
    for v in range(2):
        collect(1, v)
        x = thirds(whole[1, v])
        end = dot(x[0], order[...]) + (dot(x[1], order[...]) + dot(x[2], order[...]))
        for r in range(4):
            out[v, :, r, :] = end[:levels, r * 128 : (r + 1) * 128]

    for s, source in ((0, src), (1, seen)):
        for v in range(2):
            for d in (1, 2, 3):
                scatter_copy(s, source, d, v).wait_send()
            for k in range(WINDOWS):
                @pl.when(t != k)
                def _():
                    remote(ends.at[s, k, v], whole.at[s, v, :, mine], send_e.at[s, k, v],
                           recv_e.at[s, t, v], (k, b)).wait_send()
    for copy in started:
        copy.wait_send()

    def drain(d):
        return_copy(d).wait_send()
        profile_copy(d).wait_send()

    loop(0, bands - 1, drain)


def run(bands, f, coupling, diff, picks, weights, counts, errors, jac):
    vmem = pl.BlockSpec(memory_space=pltpu.VMEM)
    dma = pltpu.SemaphoreType.DMA
    slots = bands * jac.shape[2]
    packed = pltpu.VMEM((bands, 40, 128), F32)
    return pl.pallas_call(
        functools.partial(whole_loop, bands),
        out_shape=jax.ShapeDtypeStruct(f.shape, F32),
        in_specs=[pl.BlockSpec(memory_space=pl.ANY)] * 8,
        out_specs=vmem,
        scratch_shapes=[
            pltpu.VMEM(x.shape, x.dtype)
            for x in (f, coupling, diff, picks, weights, counts, errors)
        ] + [
            dma((7,)),
            pltpu.VMEM((REGION, REGION), BF16),
            pltpu.VMEM((2, SPAN, REGION), F32),
            pltpu.VMEM((2, WINDOWS, 2, SPAN, TILE), F32),
            pltpu.VMEM((2, WINDOWS, 2, SPAN, REGION), F32),
            pltpu.VMEM((2, WINDOWS, 2, 64, 256), F32),
            pltpu.VMEM((2, WINDOWS, 2, 128, 256), F32),
            pltpu.VMEM((2, WINDOWS, 2, SPAN, TILE), F32),
            pltpu.VMEM((3, 2, SPAN, REGION), F32),
            pltpu.VMEM((2, 4, 128), F32),
            pltpu.VMEM((REGION, REGION), F32),
            pltpu.VMEM((256, 256), F32),
            pltpu.VMEM((2, 2, SPAN, SPAN), BF16),
            pltpu.VMEM((2, 2, REGION, TILE), BF16),
            pltpu.VMEM(jac.shape, F32),
            pltpu.VMEM(jac.shape, F32),
            pltpu.VMEM((2, slots, REGION), BF16),
            packed, packed, packed, packed,
            dma((2, 2, 4)), dma((2, 4, 2)),
            dma((2, 4, 2, 8)), dma((2, 4, 2, 8)),
            dma((2, 4, 2)), dma((2, 4, 2)),
            dma((2,)), dma((2,)),
            dma((bands,)), dma((bands,)), dma((bands,)), dma((bands,)), dma((bands,)),
        ],
        compiler_params=pltpu.CompilerParams(
            collective_id=0, has_side_effects=True, vmem_limit_bytes=56 * 1024 * 1024,
        ),
        name="inner_loop",
    )(f, coupling, diff, picks, weights, counts, errors, jac)


def shards(forcing, coupling, diffusion, error_scale, pick_cols, pick_weights,
           send_count, jacobian, obs_weight):
    own = forcing[0]
    adjoint = run(
        lax.axis_size("lat"), own, coupling, diffusion,
        jnp.transpose(pick_cols[0, 0], (1, 2, 0)),
        jnp.transpose(pick_weights[0, 0], (1, 2, 0)),
        send_count[0],
        jnp.transpose(obs_weight[0, 0], (2, 1, 0)),
        jnp.transpose(jacobian[0, 0], (0, 2, 1, 3)),
    )
    return (adjoint + error_scale[None, :, None, None] * own)[None]


def solution(mesh):
    return jax.shard_map(
        shards,
        mesh=mesh,
        in_specs=(
            P("tm", None, None, "lat", None),
            P(),
            P("lat", None),
            P(),
            P("tm", "lat", None, None, None),
            P("tm", "lat", None, None, None),
            P("tm", "lat", None),
            P("tm", "lat", None, None, None, None),
            P("tm", "lat", None, None, None),
        ),
        out_specs=P("tm", None, None, "lat", None),
        check_vma=False,
    )
```

```python
import functools
import jax
import jax.numpy as jnp
from jax import lax
from jax.experimental import pallas as pl
from jax.experimental.pallas import tpu as pltpu
from jax.sharding import PartitionSpec as P

F32 = jnp.float32
BF16 = jnp.bfloat16
MESH = pl.DeviceIdType.MESH
HIGHEST = lax.Precision.HIGHEST
TILE = 128
REGION = 512
FIELDS = 288
SPAN = 144
WINDOWS = 4

NN = ((1,), (0,))
NT = ((1,), (1,))


def dot(a, b, dims=NN, precision=None):
    return lax.dot_general(
        a, b, (dims, ((), ())), precision=precision, preferred_element_type=F32
    )


def halves(x):
    high = x.astype(BF16)
    return high, (x - high.astype(F32)).astype(BF16)


def thirds(x):
    high = x.astype(BF16)
    rest = x - high.astype(F32)
    middle = rest.astype(BF16)
    return high, middle, (rest - middle.astype(F32)).astype(BF16)


def dot3(a, b, dims=NN):
    return dot(a[0], b[0], dims) + (dot(a[0], b[1], dims) + dot(a[1], b[0], dims))


def band_column(i):
    return ((i >> 2) & 3) * 128 + (i >> 7) * 32 + ((i >> 4) & 7) * 4 + (i & 3)


def corner_cell(j):
    down = jnp.where(j < 3, 1, jnp.where(j < 5, 2, 3))
    return down, jnp.where(j < 3, j + 1, jnp.where(j < 5, j - 2, j - 4))


def region_place(i):
    block = i >> 7
    row = ((i >> 2) & 3) + jnp.where(block == 1, -4, jnp.where(block == 2, 4, 0))
    lon = ((i >> 4) & 7) * 4 + (i & 3)
    k = i - 384
    side_lon = (i & 3) + jnp.where(k < 16, -4, 32)
    corner = (k - 32) >> 3
    dr, dl = corner_cell(k & 7)
    corner_row = jnp.where(corner < 2, -dr, 3 + dr)
    corner_lon = jnp.where((corner & 1) == 0, -dl, 31 + dl)
    row = jnp.where(i < 416, jnp.where(i < 384, row, (i >> 2) & 3), corner_row)
    return row, jnp.where(i < 384, lon, jnp.where(i < 416, side_lon, corner_lon))


def region_used(i):
    return (i < 416) | ((i < 448) & ((i & 7) < 6))


def edge_column(i):
    side = jnp.where(i < 16, i, i + 96)
    corner = (i - 32) >> 3
    dr, dl = corner_cell(i & 7)
    row = jnp.where(corner < 2, 4 - dr, dr - 1)
    lon = jnp.where((corner & 1) == 0, 32 - dl, dl - 1)
    return jnp.where(i < 32, side, (lon >> 2) * 16 + row * 4 + (lon & 3))


def step_matrix(bands, band, part, above, here, below):
    i = lax.broadcasted_iota(jnp.int32, (REGION, 128), 0)
    lane = lax.broadcasted_iota(jnp.int32, (REGION, 128), 1)
    row_i, lon_i = region_place(i)
    rows = jnp.zeros((REGION, 128), F32)
    for source, first in ((above, -4), (here, 0), (below, 4)):
        for k in range(4):
            rows = jnp.where(row_i == first + k, source[k : k + 1, :], rows)
    picked = lane == ((lon_i + 32 * part) & 127)
    spread = jnp.sum(jnp.where(picked, rows, 0.0), axis=1, keepdims=True)
    i1 = lax.broadcasted_iota(jnp.int32, (REGION, 1), 0)
    j1 = lax.broadcasted_iota(jnp.int32, (1, REGION), 1)
    row_a, lon_a = region_place(i1)
    row_b, lon_b = region_place(j1)
    last = 4 * bands - 4 * band
    ok_a = (row_a >= -4 * band) & (row_a < last) & region_used(i1)
    ok_b = (row_b >= -4 * band) & (row_b < last) & region_used(j1)
    spread = jnp.where(ok_a, spread, 0.0)
    one = jnp.where(ok_a, 1.0, 0.0)
    apart = jnp.abs(row_a - row_b) + jnp.abs(lon_a - lon_b)
    h = jnp.where(apart == 0, one - 4.0 * spread, jnp.where(apart == 1, spread, 0.0))
    return jnp.where(ok_b, h, 0.0)


EDGES = (
    (32, 32, 8, 1, 1),
    (40, 40, 8, 1, -1),
    (48, 48, 8, -1, 1),
    (56, 56, 8, -1, -1),
    (0, 16, 16, 0, 1),
    (16, 0, 16, 0, -1),
)


def whole_loop(bands, f_hbm, coupling_hbm, diff_hbm, picks_hbm, weights_hbm, counts_hbm, errors_hbm,
               balance_hbm, jac, out, f, coupling, diff, picks, weights, counts, errors, balance, fetched, order, src, parts, region, own_edges, edges, ends, whole, dbuf, hmat, power,
               mixer, table, jbuf, jscaled, select, prof_out, prof_in, ret_out, ret_in,
               send_x, recv_x, send_h, recv_h, send_e, recv_e, send_d, recv_d,
               jsem, send_p, recv_p, send_r, recv_r):
    t, b = lax.axis_index("tm"), lax.axis_index("lat")
    channels, cap, levels = jac.shape[1:]
    mine = pl.ds(pl.multiple_of(t * TILE, TILE), TILE)

    def place(dt, db):
        return (lax.rem(t + dt + WINDOWS, WINDOWS), lax.rem(b + db + bands, bands))

    def band_at(d):
        return lax.rem(b + d + bands, bands)

    def remote(source, target, send, recv, device):
        return pltpu.make_async_remote_copy(
            src_ref=source, dst_ref=target, send_sem=send, recv_sem=recv,
            device_id=device, device_id_type=MESH,
        )

    def loop(first, last, body):
        def step(d, carry):
            body(d)
            return carry

        lax.fori_loop(first, last, step, 0)

    barrier = pltpu.get_barrier_semaphore()
    greeted = [(d, 0) for d in (1, 2, 3)] + [(d, s) for d in (-1, 1) for s in (-1, 1)]
    for dt, db in greeted:
        pl.semaphore_signal(barrier, inc=1, device_id=place(dt, db), device_id_type=MESH)
    loop(1, bands, lambda d: pl.semaphore_signal(
        barrier, inc=1, device_id=(t, band_at(d)), device_id_type=MESH))

    fetches = []
    for k, (source, target) in enumerate((
            (f_hbm, f), (coupling_hbm, coupling), (diff_hbm, diff), (picks_hbm, picks),
            (weights_hbm, weights), (counts_hbm, counts), (errors_hbm, errors),
            (balance_hbm, balance))):
        fetches.append(pltpu.make_async_copy(source, target, fetched.at[k]))
        fetches[-1].start()

    def jac_copy(q):
        return pltpu.make_async_copy(jac.at[q], jbuf.at[q], jsem.at[q])

    loop(0, bands, lambda q: jac_copy(q).start())

    place_i = band_column(lax.broadcasted_iota(jnp.int32, (REGION, 1), 0))
    column = lax.broadcasted_iota(jnp.int32, (1, REGION), 1)
    order[...] = (place_i == column).astype(F32).astype(BF16)
    for copy in fetches:
        copy.wait()
    for v in range(2):
        src[v, 136:, :] = jnp.zeros((8, REGION), F32)
        for r in range(4):
            src[v, :levels, r * 128 : (r + 1) * 128] = f[v, :, r, :]
        x = thirds(src[v])
        src[v] = dot(x[0], order[...], NT) + (dot(x[1], order[...], NT) + dot(x[2], order[...], NT))

    pl.semaphore_wait(barrier, len(greeted) + bands - 1)

    spreads = [remote(diff, dbuf.at[k], send_d.at[k], recv_d.at[k], place(0, s))
               for k, s in ((0, 1), (1, -1))]
    for copy in spreads:
        copy.start()

    started = []

    def scatter_copy(s, source, d, v):
        to = lax.rem(t + d, WINDOWS)
        return remote(source.at[v, :, pl.ds(pl.multiple_of(to * TILE, TILE), TILE)],
                      parts.at[s, t, v], send_x.at[s, v, d], recv_x.at[s, t, v], (to, b))

    def scatter(s, source):
        for v in range(2):
            for d in (2, 1, 3):
                scatter_copy(s, source, d, v).start()
        for v in range(2):
            parts[s, t, v] = source[v, :, mine]

    scatter(0, src)

    for s in range(2):
        for w in range(WINDOWS):
            for v in range(2):
                edges[s, w, v, 64:, :] = jnp.zeros((64, 256), F32)
    eye = (lax.broadcasted_iota(jnp.int32, (levels, levels), 0)
           == lax.broadcasted_iota(jnp.int32, (levels, levels), 1)).astype(F32)
    mix = 0.8 * eye + 0.2 * coupling[...]
    scale = jnp.sum(eye * balance[...], axis=1, keepdims=True)
    twice = dot(mix, mix, precision=HIGHEST)
    power[...] = jnp.zeros((256, 256), F32)
    power[:levels, :levels] = dot(twice, twice, precision=HIGHEST)
    for s in range(2):
        full = power[...] if s == 0 else jnp.swapaxes(power[...], 0, 1)
        high, low = halves(full[:SPAN, :SPAN])
        mixer[s, 0] = high
        mixer[s, 1] = low

    def ahead_table():
        for copy in spreads:
            copy.wait()
        hmat[...] = step_matrix(bands, b, t, dbuf[0], diff[...], dbuf[1])
        g = hmat[:TILE, :]
        for _ in range(3):
            g = dot(g, hmat[...], precision=HIGHEST)
        high, low = halves(jnp.swapaxes(g, 0, 1))
        table[0, 0] = high
        table[0, 1] = low

    edge_i = edge_column(lax.broadcasted_iota(jnp.int32, (64, TILE), 0))
    edge_j = lax.broadcasted_iota(jnp.int32, (64, TILE), 1)
    edge_of = (edge_j == edge_i).astype(F32).astype(BF16)

    def halo_copies(s, w, v):
        copies = []
        for k, (at, start, size, db, dt) in enumerate(EDGES):
            copies.append(remote(own_edges.at[s, w, v, pl.ds(start, size)],
                                 edges.at[s, w, v, pl.ds(at, size)],
                                 send_h.at[s, w, v, k], recv_h.at[s, w, v, k], place(dt, db)))
        for k, db in ((1, 1), (2, -1)):
            copies.append(remote(region.at[s, w, v, :, pl.ds(0, TILE)],
                                 region.at[s, w, v, :, pl.ds(k * TILE, TILE)],
                                 send_h.at[s, w, v, 5 + k], recv_h.at[s, w, v, 5 + k], place(0, db)))
        return copies

    def send_halo(s, w, before, v):
        @pl.when(t != w)
        def _():
            remote(parts.at[s, w, v], parts.at[s, w, v], send_x.at[s, v, 0], recv_x.at[s, w, v],
                   (t, b)).wait_recv()

        state = parts[s, w, v]
        if before is not None:
            state = state + ends[s, before, v]
        mixed = dot3((mixer[s, 0], mixer[s, 1]), halves(state))
        center = halves(mixed)
        own_edges[s, w, v, :, :SPAN] = dot(edge_of, center[0], NT) + dot(edge_of, center[1], NT)
        region[s, w, v, :, :TILE] = mixed
        copies = halo_copies(s, w, v)
        for copy in copies:
            copy.start()
        started.extend(copies)

    def receive_halo(s, w, v):
        for copy in halo_copies(s, w, v):
            copy.wait_recv()
        region[s, w, v, :, 384:] = jnp.swapaxes(edges[s, w, v], 0, 1)[:SPAN]
        ends[s, w, v] = dot3(halves(region[s, w, v]), (table[s, 0], table[s, 1]))

    def send_end(s, w, v):
        @pl.when(t != w)
        def _():
            remote(ends.at[s, w, v], whole.at[s, v, :, mine], send_e.at[s, w, v],
                   recv_e.at[s, t, v], (w, b)).start()

        @pl.when(t == w)
        def _():
            whole[s, v, :, mine] = ends[s, w, v]

    def chain(s, windows, beside):
        for v in range(2):
            send_halo(s, windows[0], None, v)
        for k, w in enumerate(windows):
            if beside[k] is not None:
                beside[k]()
            for v in range(2):
                receive_halo(s, w, v)
                if k < WINDOWS - 1:
                    send_halo(s, windows[k + 1], w, v)
                else:
                    send_end(s, w, v)
        for w in windows[-2::-1]:
            for v in range(2):
                send_end(s, w, v)

    def collect(s, v):
        for k in range(WINDOWS):
            @pl.when(t != k)
            def _():
                piece = whole.at[s, v, :, pl.ds(k * TILE, TILE)]
                remote(piece, piece, send_e.at[s, k, v], recv_e.at[s, k, v], (t, b)).wait_recv()

    slots = bands * cap

    def make_select():
        slot = lax.broadcasted_iota(jnp.int32, (slots, bands), 0)
        owner = lax.broadcasted_iota(jnp.int32, (slots, bands), 1)
        spread = (slot // cap == owner).astype(F32)
        near = picks.shape[1]
        row = lax.broadcasted_iota(jnp.int32, (slots, cap * near), 0)
        lane = lax.broadcasted_iota(jnp.int32, (slots, cap * near), 1)
        own = lane // near == row % cap
        chosen = jnp.zeros((slots, REGION), F32)
        col = jnp.concatenate([picks[c] for c in range(cap)], axis=0).astype(F32)
        wt = jnp.concatenate([jnp.where(counts[...] > c, weights[c], 0.0) for c in range(cap)], axis=0)
        col = dot(spread, col, NT, HIGHEST)
        wt = dot(spread, wt, NT, HIGHEST)
        at = band_column(lax.broadcasted_iota(jnp.int32, (1, REGION), 1)).astype(F32)
        for k in range(near):
            here = own & (lane % near == k)
            col_k = jnp.sum(jnp.where(here, col, 0.0), axis=1, keepdims=True)
            wt_k = jnp.sum(jnp.where(here, wt, 0.0), axis=1, keepdims=True)
            chosen += jnp.where(jnp.abs(col_k - at) < 0.5, wt_k, 0.0)
        high, low = halves(chosen)
        select[0] = high
        select[1] = low

    def scale_jac(first, last):
        lane = lax.broadcasted_iota(jnp.int32, (cap, bands), 1)

        def body(q):
            jac_copy(q).wait()
            for n in range(channels):
                scale = jnp.sum(jnp.where(lane == q, errors[n], 0.0), axis=1, keepdims=True)
                jscaled[q, n] = jbuf[q, n] * scale

        loop(first, last, body)

    def back_table():
        g = hmat[:, :TILE]
        for _ in range(3):
            g = dot(hmat[...], g, precision=HIGHEST)
        high, low = halves(g)
        table[1, 0] = high
        table[1, 1] = low

    chain(0, (0, 1, 2, 3), [
        ahead_table, make_select, lambda: scale_jac(0, bands), back_table])

    def fold(x):
        count = x.shape[0] // cap
        x = x.reshape(count, cap, 384)
        last = x[:, :8, 256:] + pltpu.roll(x[:, 8:, 256:].reshape(count * 8, 128), 64, 1).reshape(count, 8, 128)
        return jnp.concatenate([x[:, :, :128], x[:, :, 128:256], last], axis=1)

    def unfold(x):
        count = x.shape[0]
        last = x[:, 2 * cap :]
        turned = pltpu.roll(last.reshape(count * 8, 128), 64, 1).reshape(count, 8, 128)
        last = jnp.concatenate([last, turned], axis=1)
        return jnp.concatenate([x[:, :cap], x[:, cap : 2 * cap], last], axis=2).reshape(count * cap, 384)

    collect(0, 0)
    collect(0, 1)
    high, low = halves(whole[0].reshape(FIELDS, REGION))
    spare = jnp.zeros((384 - FIELDS, REGION), BF16)
    state = (jnp.concatenate([high, spare], axis=0), jnp.concatenate([low, spare], axis=0))
    prof_out[...] = fold(dot3((select[0], select[1]), state, NT))

    across = min(4, bands // 2)
    down = bands // (2 * across)

    def far_first(j, size):
        if size == 4:
            return lax.rem(2 + 3 * j + 3 * (j * (j - 1) // 2), 4)
        return size - 1 - j

    def partner(d, sign):
        core = lax.rem(b + d + 1, 2)
        dy = far_first(lax.rem(d // 2, across), across)
        dx = far_first(d // (2 * across), down)
        y = lax.rem(lax.rem(b // 2, across) + sign * dy + across, across)
        x = lax.rem(b // (2 * across) + sign * dx + down, down)
        return (x * across + y) * 2 + core

    def profile_copy(d):
        q = partner(d, 1)
        return remote(prof_out.at[q], prof_in.at[b], send_p.at[d], recv_p.at[d], (t, q))

    def profile_arrival(d):
        q = partner(d, -1)
        return remote(prof_out.at[q], prof_in.at[q], send_p.at[d], recv_p.at[d], (t, q))

    def return_copy(d):
        q = partner(d, -1)
        return remote(ret_out.at[q], ret_in.at[b], send_r.at[d], recv_r.at[d], (t, q))

    def return_arrival(d):
        q = partner(d, 1)
        return remote(ret_out.at[q], ret_in.at[q], send_r.at[d], recv_r.at[d], (t, q))

    profile_copy(bands - 2).start()
    loop(0, bands - 2, lambda d: profile_copy(d).start())

    def work(q, packed):
        profile = unfold(packed[None])
        first = profile[:, :levels]
        second = pltpu.roll(profile[:, 128:], 256 - (SPAN - 128), 1)[:, :levels]
        sums = [jnp.zeros((cap, levels), F32)] * 2
        for n in range(channels):
            jn, jw = jbuf[q, n], jscaled[q, n]
            for v, p in enumerate((first, second)):
                hidden = jnp.sum(jn * p, axis=1, keepdims=True)
                sums[v] = sums[v] + jw * hidden
        spare = jnp.zeros((cap, 256 - levels), F32)
        one = jnp.concatenate([sums[0], spare], axis=1)
        two = pltpu.roll(jnp.concatenate([sums[1], spare], axis=1), SPAN - 128, 1)
        back = jnp.concatenate([one[:, :128], one[:, 128:] + two[:, :128], two[:, 128:]], axis=1)
        return fold(back)[0]

    ret_in[b] = work(b, prof_out[b])

    def serve(d):
        q = partner(d, -1)
        profile_arrival(d).wait_recv()
        ret_out[q] = work(q, prof_in[q])
        return_copy(d).start()

    serve(bands - 2)
    loop(0, bands - 2, serve)
    loop(0, bands - 1, lambda d: return_arrival(d).wait_recv())
    back = halves(jnp.swapaxes(unfold(ret_in[...]), 0, 1)[:FIELDS])
    seen = whole.at[2]
    seen[...] = dot3(back, (select[0], select[1])).reshape(2, SPAN, REGION)
    scatter(1, seen)
    chain(1, (3, 2, 1, 0), [None] * WINDOWS)
    for v in range(2):
        collect(1, v)
        x = thirds(whole[1, v])
        end = dot(x[0], order[...]) + (dot(x[1], order[...]) + dot(x[2], order[...]))
        for r in range(4):
            out[v, :, r, :] = end[:levels, r * 128 : (r + 1) * 128] + scale * f[v, :, r, :]

    for s, source in ((0, src), (1, seen)):
        for v in range(2):
            for d in (1, 2, 3):
                scatter_copy(s, source, d, v).wait_send()
            for k in range(WINDOWS):
                @pl.when(t != k)
                def _():
                    remote(ends.at[s, k, v], whole.at[s, v, :, mine], send_e.at[s, k, v],
                           recv_e.at[s, t, v], (k, b)).wait_send()
    for copy in started:
        copy.wait_send()

    def drain(d):
        return_copy(d).wait_send()
        profile_copy(d).wait_send()

    loop(0, bands - 1, drain)


def run(bands, f, coupling, diff, picks, weights, counts, errors, balance, jac):
    vmem = pl.BlockSpec(memory_space=pltpu.VMEM)
    dma = pltpu.SemaphoreType.DMA
    slots = bands * jac.shape[2]
    packed = pltpu.VMEM((bands, 40, 128), F32)
    return pl.pallas_call(
        functools.partial(whole_loop, bands),
        out_shape=jax.ShapeDtypeStruct(f.shape, F32),
        in_specs=[pl.BlockSpec(memory_space=pl.ANY)] * 9,
        out_specs=vmem,
        scratch_shapes=[
            pltpu.VMEM(x.shape, x.dtype)
            for x in (f, coupling, diff, picks, weights, counts, errors, balance)
        ] + [
            dma((8,)),
            pltpu.VMEM((REGION, REGION), BF16),
            pltpu.VMEM((2, SPAN, REGION), F32),
            pltpu.VMEM((2, WINDOWS, 2, SPAN, TILE), F32),
            pltpu.VMEM((2, WINDOWS, 2, SPAN, REGION), F32),
            pltpu.VMEM((2, WINDOWS, 2, 64, 256), F32),
            pltpu.VMEM((2, WINDOWS, 2, 128, 256), F32),
            pltpu.VMEM((2, WINDOWS, 2, SPAN, TILE), F32),
            pltpu.VMEM((3, 2, SPAN, REGION), F32),
            pltpu.VMEM((2, 4, 128), F32),
            pltpu.VMEM((REGION, REGION), F32),
            pltpu.VMEM((256, 256), F32),
            pltpu.VMEM((2, 2, SPAN, SPAN), BF16),
            pltpu.VMEM((2, 2, REGION, TILE), BF16),
            pltpu.VMEM(jac.shape, F32),
            pltpu.VMEM(jac.shape, F32),
            pltpu.VMEM((2, slots, REGION), BF16),
            packed, packed, packed, packed,
            dma((2, 2, 4)), dma((2, 4, 2)),
            dma((2, 4, 2, 8)), dma((2, 4, 2, 8)),
            dma((2, 4, 2)), dma((2, 4, 2)),
            dma((2,)), dma((2,)),
            dma((bands,)), dma((bands,)), dma((bands,)), dma((bands,)), dma((bands,)),
        ],
        compiler_params=pltpu.CompilerParams(
            collective_id=0, has_side_effects=True, vmem_limit_bytes=56 * 1024 * 1024,
        ),
        name="inner_loop",
    )(f, coupling, diff, picks, weights, counts, errors, balance, jac)


def shards(forcing, coupling, diffusion, error_scale, pick_cols, pick_weights,
           send_count, jacobian, obs_weight):
    own = forcing[0]
    gradient = run(
        lax.axis_size("lat"), own, coupling, diffusion,
        jnp.transpose(pick_cols[0, 0], (1, 2, 0)),
        jnp.transpose(pick_weights[0, 0], (1, 2, 0)),
        send_count[0],
        jnp.transpose(obs_weight[0, 0], (2, 1, 0)),
        error_scale[None],
        jnp.transpose(jacobian[0, 0], (0, 2, 1, 3)),
    )
    return gradient[None]


def solution(mesh):
    return jax.shard_map(
        shards,
        mesh=mesh,
        in_specs=(
            P("tm", None, None, "lat", None),
            P(),
            P("lat", None),
            P(),
            P("tm", "lat", None, None, None),
            P("tm", "lat", None, None, None),
            P("tm", "lat", None),
            P("tm", "lat", None, None, None, None),
            P("tm", "lat", None, None, None),
        ),
        out_specs=P("tm", None, None, "lat", None),
        check_vma=False,
    )
```

```python
import functools
import jax
import jax.numpy as jnp
from jax import lax
from jax.experimental import pallas as pl
from jax.experimental.pallas import tpu as pltpu
from jax.sharding import PartitionSpec as P

F32 = jnp.float32
BF16 = jnp.bfloat16
MESH = pl.DeviceIdType.MESH
HIGHEST = lax.Precision.HIGHEST
TILE = 128
REGION = 512
FIELDS = 288
SPAN = 144
WINDOWS = 4

NN = ((1,), (0,))
NT = ((1,), (1,))


def dot(a, b, dims=NN, precision=None):
    return lax.dot_general(
        a, b, (dims, ((), ())), precision=precision, preferred_element_type=F32
    )


def halves(x):
    high = x.astype(BF16)
    return high, (x - high.astype(F32)).astype(BF16)


def dot3(a, b, dims=NN):
    return dot(a[0], b[0], dims) + (dot(a[0], b[1], dims) + dot(a[1], b[0], dims))


def band_column(i):
    return ((i >> 2) & 3) * 128 + (i >> 7) * 32 + ((i >> 4) & 7) * 4 + (i & 3)


def corner_cell(j):
    down = jnp.where(j < 3, 1, jnp.where(j < 5, 2, 3))
    return down, jnp.where(j < 3, j + 1, jnp.where(j < 5, j - 2, j - 4))


def region_place(i):
    block = i >> 7
    row = ((i >> 2) & 3) + jnp.where(block == 1, -4, jnp.where(block == 2, 4, 0))
    lon = ((i >> 4) & 7) * 4 + (i & 3)
    k = i - 384
    side_lon = (i & 3) + jnp.where(k < 16, -4, 32)
    corner = (k - 32) >> 3
    dr, dl = corner_cell(k & 7)
    corner_row = jnp.where(corner < 2, -dr, 3 + dr)
    corner_lon = jnp.where((corner & 1) == 0, -dl, 31 + dl)
    row = jnp.where(i < 416, jnp.where(i < 384, row, (i >> 2) & 3), corner_row)
    return row, jnp.where(i < 384, lon, jnp.where(i < 416, side_lon, corner_lon))


def region_used(i):
    return (i < 416) | ((i < 448) & ((i & 7) < 6))


def edge_column(i):
    side = jnp.where(i < 16, i, i + 96)
    corner = (i - 32) >> 3
    dr, dl = corner_cell(i & 7)
    row = jnp.where(corner < 2, 4 - dr, dr - 1)
    lon = jnp.where((corner & 1) == 0, 32 - dl, dl - 1)
    return jnp.where(i < 32, side, (lon >> 2) * 16 + row * 4 + (lon & 3))


def step_matrix(bands, band, part, above, here, below):
    i = lax.broadcasted_iota(jnp.int32, (REGION, 128), 0)
    lane = lax.broadcasted_iota(jnp.int32, (REGION, 128), 1)
    row_i, lon_i = region_place(i)
    rows = jnp.zeros((REGION, 128), F32)
    for source, first in ((above, -4), (here, 0), (below, 4)):
        for k in range(4):
            rows = jnp.where(row_i == first + k, source[k : k + 1, :], rows)
    picked = lane == ((lon_i + 32 * part) & 127)
    spread = jnp.sum(jnp.where(picked, rows, 0.0), axis=1, keepdims=True)
    i1 = lax.broadcasted_iota(jnp.int32, (REGION, 1), 0)
    j1 = lax.broadcasted_iota(jnp.int32, (1, REGION), 1)
    row_a, lon_a = region_place(i1)
    row_b, lon_b = region_place(j1)
    last = 4 * bands - 4 * band
    ok_a = (row_a >= -4 * band) & (row_a < last) & region_used(i1)
    ok_b = (row_b >= -4 * band) & (row_b < last) & region_used(j1)
    spread = jnp.where(ok_a, spread, 0.0)
    one = jnp.where(ok_a, 1.0, 0.0)
    apart = jnp.abs(row_a - row_b) + jnp.abs(lon_a - lon_b)
    h = jnp.where(apart == 0, one - 4.0 * spread, jnp.where(apart == 1, spread, 0.0))
    return jnp.where(ok_b, h, 0.0)


EDGES = (
    (32, 32, 8, 1, 1),
    (40, 40, 8, 1, -1),
    (48, 48, 8, -1, 1),
    (56, 56, 8, -1, -1),
    (0, 16, 16, 0, 1),
    (16, 0, 16, 0, -1),
)


def whole_loop(bands, f_hbm, coupling_hbm, diff_hbm, picks_hbm, weights_hbm, counts_hbm, errors_hbm, jac, out,
               f, coupling, diff, picks, weights, counts, errors, fetched, order, src, parts, region, own_edges, edges, ends, whole, dbuf, hmat, power,
               mixer, table, jbuf, jscaled, select, prof_out, prof_in, ret_out, ret_in,
               send_x, recv_x, send_h, recv_h, send_e, recv_e, send_d, recv_d,
               jsem, send_p, recv_p, send_r, recv_r):
    t, b = lax.axis_index("tm"), lax.axis_index("lat")
    channels, cap, levels = jac.shape[1:]
    mine = pl.ds(pl.multiple_of(t * TILE, TILE), TILE)

    def place(dt, db):
        return (lax.rem(t + dt + WINDOWS, WINDOWS), lax.rem(b + db + bands, bands))

    def band_at(d):
        return lax.rem(b + d + bands, bands)

    def remote(source, target, send, recv, device):
        return pltpu.make_async_remote_copy(
            src_ref=source, dst_ref=target, send_sem=send, recv_sem=recv,
            device_id=device, device_id_type=MESH,
        )

    def loop(first, last, body):
        def step(d, carry):
            body(d)
            return carry

        lax.fori_loop(first, last, step, 0)

    barrier = pltpu.get_barrier_semaphore()
    greeted = [(d, 0) for d in (1, 2, 3)] + [(d, s) for d in (-1, 1) for s in (-1, 1)]
    for dt, db in greeted:
        pl.semaphore_signal(barrier, inc=1, device_id=place(dt, db), device_id_type=MESH)
    loop(1, bands, lambda d: pl.semaphore_signal(
        barrier, inc=1, device_id=(t, band_at(d)), device_id_type=MESH))

    fetches = []
    for k, (source, target) in enumerate((
            (f_hbm, f), (coupling_hbm, coupling), (diff_hbm, diff), (picks_hbm, picks),
            (weights_hbm, weights), (counts_hbm, counts), (errors_hbm, errors))):
        fetches.append(pltpu.make_async_copy(source, target, fetched.at[k]))
        fetches[-1].start()

    def jac_copy(q):
        return pltpu.make_async_copy(jac.at[q], jbuf.at[q], jsem.at[q])

    place_i = band_column(lax.broadcasted_iota(jnp.int32, (REGION, 1), 0))
    column = lax.broadcasted_iota(jnp.int32, (1, REGION), 1)
    order[...] = (place_i == column).astype(F32).astype(BF16)
    for copy in fetches:
        copy.wait()
    for v in range(2):
        src[v, 136:, :] = jnp.zeros((8, REGION), F32)
        for r in range(4):
            src[v, :levels, r * 128 : (r + 1) * 128] = f[v, :, r, :]
        x = halves(src[v])
        src[v] = dot(x[0], order[...], NT) + dot(x[1], order[...], NT)

    pl.semaphore_wait(barrier, len(greeted) + bands - 1)

    spreads = [remote(diff, dbuf.at[k], send_d.at[k], recv_d.at[k], place(0, s))
               for k, s in ((0, 1), (1, -1))]
    for copy in spreads:
        copy.start()

    started = []

    def scatter_copy(s, source, d, v):
        to = lax.rem(t + d, WINDOWS)
        return remote(source.at[v, :, pl.ds(pl.multiple_of(to * TILE, TILE), TILE)],
                      parts.at[s, t, v], send_x.at[s, v, d], recv_x.at[s, t, v], (to, b))

    def scatter(s, source):
        for v in range(2):
            for d in (2, 1, 3):
                scatter_copy(s, source, d, v).start()
        for v in range(2):
            parts[s, t, v] = source[v, :, mine]

    scatter(0, src)

    for s in range(2):
        for w in range(WINDOWS):
            for v in range(2):
                edges[s, w, v, 64:, :] = jnp.zeros((64, 256), F32)
    eye = (lax.broadcasted_iota(jnp.int32, (levels, levels), 0)
           == lax.broadcasted_iota(jnp.int32, (levels, levels), 1)).astype(F32)
    mix = 0.8 * eye + 0.2 * coupling[...]
    twice = dot(mix, mix, precision=HIGHEST)
    power[...] = jnp.zeros((256, 256), F32)
    power[:levels, :levels] = dot(twice, twice, precision=HIGHEST)
    for s in range(2):
        full = power[...] if s == 0 else jnp.swapaxes(power[...], 0, 1)
        high, low = halves(full[:SPAN, :SPAN])
        mixer[s, 0] = high
        mixer[s, 1] = low

    def ahead_table():
        loop(0, bands, lambda q: jac_copy(q).start())
        for copy in spreads:
            copy.wait()
        hmat[...] = step_matrix(bands, b, t, dbuf[0], diff[...], dbuf[1])
        g = hmat[:TILE, :]
        for _ in range(3):
            g = dot(g, hmat[...], precision=HIGHEST)
        high, low = halves(jnp.swapaxes(g, 0, 1))
        table[0, 0] = high
        table[0, 1] = low

    edge_i = edge_column(lax.broadcasted_iota(jnp.int32, (64, TILE), 0))
    edge_j = lax.broadcasted_iota(jnp.int32, (64, TILE), 1)
    edge_of = (edge_j == edge_i).astype(F32).astype(BF16)

    def halo_copies(s, w, v):
        copies = []
        for k, (at, start, size, db, dt) in enumerate(EDGES):
            copies.append(remote(own_edges.at[s, w, v, pl.ds(start, size)],
                                 edges.at[s, w, v, pl.ds(at, size)],
                                 send_h.at[s, w, v, k], recv_h.at[s, w, v, k], place(dt, db)))
        for k, db in ((1, 1), (2, -1)):
            copies.append(remote(region.at[s, w, v, :, pl.ds(0, TILE)],
                                 region.at[s, w, v, :, pl.ds(k * TILE, TILE)],
                                 send_h.at[s, w, v, 5 + k], recv_h.at[s, w, v, 5 + k], place(0, db)))
        return copies

    def send_halo(s, w, before, v):
        @pl.when(t != w)
        def _():
            remote(parts.at[s, w, v], parts.at[s, w, v], send_x.at[s, v, 0], recv_x.at[s, w, v],
                   (t, b)).wait_recv()

        state = parts[s, w, v]
        if before is not None:
            state = state + ends[s, before, v]
        mixed = dot3((mixer[s, 0], mixer[s, 1]), halves(state))
        center = halves(mixed)
        own_edges[s, w, v, :, :SPAN] = dot(edge_of, center[0], NT) + dot(edge_of, center[1], NT)
        region[s, w, v, :, :TILE] = mixed
        copies = halo_copies(s, w, v)
        for copy in copies:
            copy.start()
        started.extend(copies)

    def receive_halo(s, w, v):
        for copy in halo_copies(s, w, v):
            copy.wait_recv()
        region[s, w, v, :, 384:] = jnp.swapaxes(edges[s, w, v], 0, 1)[:SPAN]
        ends[s, w, v] = dot3(halves(region[s, w, v]), (table[s, 0], table[s, 1]))

    def send_end(s, w, v):
        @pl.when(t != w)
        def _():
            remote(ends.at[s, w, v], whole.at[s, v, :, mine], send_e.at[s, w, v],
                   recv_e.at[s, t, v], (w, b)).start()

        @pl.when(t == w)
        def _():
            whole[s, v, :, mine] = ends[s, w, v]

    def chain(s, windows, beside):
        for v in range(2):
            send_halo(s, windows[0], None, v)
        for k, w in enumerate(windows):
            if beside[k] is not None:
                beside[k]()
            for v in range(2):
                receive_halo(s, w, v)
                if k < WINDOWS - 1:
                    send_halo(s, windows[k + 1], w, v)
                else:
                    send_end(s, w, v)
        for w in windows[-2::-1]:
            for v in range(2):
                send_end(s, w, v)

    def collect(s, v):
        for k in range(WINDOWS):
            @pl.when(t != k)
            def _():
                piece = whole.at[s, v, :, pl.ds(k * TILE, TILE)]
                remote(piece, piece, send_e.at[s, k, v], recv_e.at[s, k, v], (t, b)).wait_recv()

    slots = bands * cap

    def make_select():
        slot = lax.broadcasted_iota(jnp.int32, (slots, bands), 0)
        owner = lax.broadcasted_iota(jnp.int32, (slots, bands), 1)
        spread = (slot // cap == owner).astype(F32)
        near = picks.shape[1]
        row = lax.broadcasted_iota(jnp.int32, (slots, cap * near), 0)
        lane = lax.broadcasted_iota(jnp.int32, (slots, cap * near), 1)
        own = lane // near == row % cap
        chosen = jnp.zeros((slots, REGION), F32)
        col = jnp.concatenate([picks[c] for c in range(cap)], axis=0).astype(F32)
        wt = jnp.concatenate([jnp.where(counts[...] > c, weights[c], 0.0) for c in range(cap)], axis=0)
        col = dot(spread, col, NT, HIGHEST)
        wt = dot(spread, wt, NT, HIGHEST)
        at = band_column(lax.broadcasted_iota(jnp.int32, (1, REGION), 1)).astype(F32)
        for k in range(near):
            here = own & (lane % near == k)
            col_k = jnp.sum(jnp.where(here, col, 0.0), axis=1, keepdims=True)
            wt_k = jnp.sum(jnp.where(here, wt, 0.0), axis=1, keepdims=True)
            chosen += jnp.where(jnp.abs(col_k - at) < 0.5, wt_k, 0.0)
        high, low = halves(chosen)
        select[0] = high
        select[1] = low

    def scale_jac(first, last):
        lane = lax.broadcasted_iota(jnp.int32, (cap, bands), 1)

        def body(q):
            jac_copy(q).wait()
            for n in range(channels):
                scale = jnp.sum(jnp.where(lane == q, errors[n], 0.0), axis=1, keepdims=True)
                jscaled[q, n] = jbuf[q, n] * scale

        loop(first, last, body)

    def back_table():
        g = hmat[:, :TILE]
        for _ in range(3):
            g = dot(hmat[...], g, precision=HIGHEST)
        high, low = halves(g)
        table[1, 0] = high
        table[1, 1] = low

    chain(0, (0, 1, 2, 3), [
        ahead_table, make_select, lambda: scale_jac(0, bands), back_table])

    def fold(x):
        count = x.shape[0] // cap
        x = x.reshape(count, cap, 384)
        last = x[:, :8, 256:] + pltpu.roll(x[:, 8:, 256:].reshape(count * 8, 128), 64, 1).reshape(count, 8, 128)
        return jnp.concatenate([x[:, :, :128], x[:, :, 128:256], last], axis=1)

    def unfold(x):
        count = x.shape[0]
        last = x[:, 2 * cap :]
        turned = pltpu.roll(last.reshape(count * 8, 128), 64, 1).reshape(count, 8, 128)
        last = jnp.concatenate([last, turned], axis=1)
        return jnp.concatenate([x[:, :cap], x[:, cap : 2 * cap], last], axis=2).reshape(count * cap, 384)

    collect(0, 0)
    collect(0, 1)
    high, low = halves(whole[0].reshape(FIELDS, REGION))
    spare = jnp.zeros((384 - FIELDS, REGION), BF16)
    state = (jnp.concatenate([high, spare], axis=0), jnp.concatenate([low, spare], axis=0))
    prof_out[...] = fold(dot3((select[0], select[1]), state, NT))

    across = min(4, bands // 2)
    down = bands // (2 * across)

    def far_first(j, size):
        if size == 4:
            return lax.rem(2 + 3 * j + 3 * (j * (j - 1) // 2), 4)
        return size - 1 - j

    def partner(d, sign):
        core = lax.rem(b + d + 1, 2)
        dy = far_first(lax.rem(d // 2, across), across)
        dx = far_first(d // (2 * across), down)
        y = lax.rem(lax.rem(b // 2, across) + sign * dy + across, across)
        x = lax.rem(b // (2 * across) + sign * dx + down, down)
        return (x * across + y) * 2 + core

    def profile_copy(d):
        q = partner(d, 1)
        return remote(prof_out.at[q], prof_in.at[b], send_p.at[d], recv_p.at[d], (t, q))

    def profile_arrival(d):
        q = partner(d, -1)
        return remote(prof_out.at[q], prof_in.at[q], send_p.at[d], recv_p.at[d], (t, q))

    def return_copy(d):
        q = partner(d, -1)
        return remote(ret_out.at[q], ret_in.at[b], send_r.at[d], recv_r.at[d], (t, q))

    def return_arrival(d):
        q = partner(d, 1)
        return remote(ret_out.at[q], ret_in.at[q], send_r.at[d], recv_r.at[d], (t, q))

    profile_copy(bands - 2).start()
    loop(0, bands - 2, lambda d: profile_copy(d).start())

    def work(q, packed):
        profile = unfold(packed[None])
        first = profile[:, :levels]
        second = pltpu.roll(profile[:, 128:], 256 - (SPAN - 128), 1)[:, :levels]
        sums = [jnp.zeros((cap, levels), F32)] * 2
        for n in range(channels):
            jn, jw = jbuf[q, n], jscaled[q, n]
            for v, p in enumerate((first, second)):
                hidden = jnp.sum(jn * p, axis=1, keepdims=True)
                sums[v] = sums[v] + jw * hidden
        spare = jnp.zeros((cap, 256 - levels), F32)
        one = jnp.concatenate([sums[0], spare], axis=1)
        two = pltpu.roll(jnp.concatenate([sums[1], spare], axis=1), SPAN - 128, 1)
        back = jnp.concatenate([one[:, :128], one[:, 128:] + two[:, :128], two[:, 128:]], axis=1)
        return fold(back)[0]

    ret_in[b] = work(b, prof_out[b])

    def serve(d):
        q = partner(d, -1)
        profile_arrival(d).wait_recv()
        ret_out[q] = work(q, prof_in[q])
        return_copy(d).start()

    serve(bands - 2)
    loop(0, bands - 2, serve)
    loop(0, bands - 1, lambda d: return_arrival(d).wait_recv())
    back = halves(jnp.swapaxes(unfold(ret_in[...]), 0, 1)[:FIELDS])
    seen = whole.at[2]
    seen[...] = dot3(back, (select[0], select[1])).reshape(2, SPAN, REGION)
    scatter(1, seen)
    chain(1, (3, 2, 1, 0), [None] * WINDOWS)
    for v in range(2):
        collect(1, v)
        x = halves(whole[1, v])
        end = dot(x[0], order[...]) + dot(x[1], order[...])
        for r in range(4):
            out[v, :, r, :] = end[:levels, r * 128 : (r + 1) * 128]

    for s, source in ((0, src), (1, seen)):
        for v in range(2):
            for d in (1, 2, 3):
                scatter_copy(s, source, d, v).wait_send()
            for k in range(WINDOWS):
                @pl.when(t != k)
                def _():
                    remote(ends.at[s, k, v], whole.at[s, v, :, mine], send_e.at[s, k, v],
                           recv_e.at[s, t, v], (k, b)).wait_send()
    for copy in started:
        copy.wait_send()

    def drain(d):
        return_copy(d).wait_send()
        profile_copy(d).wait_send()

    loop(0, bands - 1, drain)


def run(bands, f, coupling, diff, picks, weights, counts, errors, jac):
    vmem = pl.BlockSpec(memory_space=pltpu.VMEM)
    dma = pltpu.SemaphoreType.DMA
    slots = bands * jac.shape[2]
    packed = pltpu.VMEM((bands, 40, 128), F32)
    return pl.pallas_call(
        functools.partial(whole_loop, bands),
        out_shape=jax.ShapeDtypeStruct(f.shape, F32),
        in_specs=[pl.BlockSpec(memory_space=pl.ANY)] * 8,
        out_specs=vmem,
        scratch_shapes=[
            pltpu.VMEM(x.shape, x.dtype)
            for x in (f, coupling, diff, picks, weights, counts, errors)
        ] + [
            dma((7,)),
            pltpu.VMEM((REGION, REGION), BF16),
            pltpu.VMEM((2, SPAN, REGION), F32),
            pltpu.VMEM((2, WINDOWS, 2, SPAN, TILE), F32),
            pltpu.VMEM((2, WINDOWS, 2, SPAN, REGION), F32),
            pltpu.VMEM((2, WINDOWS, 2, 64, 256), F32),
            pltpu.VMEM((2, WINDOWS, 2, 128, 256), F32),
            pltpu.VMEM((2, WINDOWS, 2, SPAN, TILE), F32),
            pltpu.VMEM((3, 2, SPAN, REGION), F32),
            pltpu.VMEM((2, 4, 128), F32),
            pltpu.VMEM((REGION, REGION), F32),
            pltpu.VMEM((256, 256), F32),
            pltpu.VMEM((2, 2, SPAN, SPAN), BF16),
            pltpu.VMEM((2, 2, REGION, TILE), BF16),
            pltpu.VMEM(jac.shape, F32),
            pltpu.VMEM(jac.shape, F32),
            pltpu.VMEM((2, slots, REGION), BF16),
            packed, packed, packed, packed,
            dma((2, 2, 4)), dma((2, 4, 2)),
            dma((2, 4, 2, 8)), dma((2, 4, 2, 8)),
            dma((2, 4, 2)), dma((2, 4, 2)),
            dma((2,)), dma((2,)),
            dma((bands,)), dma((bands,)), dma((bands,)), dma((bands,)), dma((bands,)),
        ],
        compiler_params=pltpu.CompilerParams(
            collective_id=0, has_side_effects=True, vmem_limit_bytes=56 * 1024 * 1024,
        ),
        name="inner_loop",
    )(f, coupling, diff, picks, weights, counts, errors, jac)


def shards(forcing, coupling, diffusion, error_scale, pick_cols, pick_weights,
           send_count, jacobian, obs_weight):
    own = forcing[0]
    adjoint = run(
        lax.axis_size("lat"), own, coupling, diffusion,
        jnp.transpose(pick_cols[0, 0], (1, 2, 0)),
        jnp.transpose(pick_weights[0, 0], (1, 2, 0)),
        send_count[0],
        jnp.transpose(obs_weight[0, 0], (2, 1, 0)),
        jnp.transpose(jacobian[0, 0], (0, 2, 1, 3)),
    )
    return (adjoint + error_scale[None, :, None, None] * own)[None]


def solution(mesh):
    return jax.shard_map(
        shards,
        mesh=mesh,
        in_specs=(
            P("tm", None, None, "lat", None),
            P(),
            P("lat", None),
            P(),
            P("tm", "lat", None, None, None),
            P("tm", "lat", None, None, None),
            P("tm", "lat", None),
            P("tm", "lat", None, None, None, None),
            P("tm", "lat", None, None, None),
        ),
        out_specs=P("tm", None, None, "lat", None),
        check_vma=False,
    )
```
